512 devices in a mesh: lab: 32 (over z_lo, y, core), img: 16 (over x, z_hi).
Axes of the slice: x: 4, y: 4, z: 16 (z_hi: 4, z_lo: 4; z = z_hi * 4 + z_lo), core: 2. Of those that a mesh axis runs over, the one named last changes fastest.
Arguments:
- queries: bfloat16 [32768, 512], P('lab'), may hold values from -12 to 12
- keys: bfloat16 [16, 576, 512], P('img', 'lab'), may hold values from -5 to 5
- values: bfloat16 [16, 576, 512], P('img', 'lab'), may hold values from -6 to 6
- grad_out: bfloat16 [16, 32768, 512], P('img', 'lab'), may hold values from -6 to 6
- block_mask: int32 [256, 16], P('lab', 'img'), may hold values from 0 to 1, as said below
Outputs:
- grad_queries: bfloat16 [32768, 512], P(('lab', 'img'))
- grad_keys: bfloat16 [16, 576, 512], P('img', 'lab')
- grad_values: bfloat16 [16, 576, 512], P('img', 'lab')
The draws below stay inside these ranges and needn't reach their ends.
Inputs may be any that keep to these rules, and one draw needn't show every extreme that they name: `block_mask`: each label block has its own density of images that it reads.
All inputs are finite; a program needn't handle non-finite values.
Results may differ from the reference program's by a relative error of at most 0.0061.
Values may be sent and summed in bfloat16 or wider, within the bound.
A program may use at most 128 MiB of HBM per device.

```python
import math
import jax
import jax.numpy as jnp
from jax import lax

H = 8
E = 64
P_SIZE = 576
BLK = 128
IMG_DEV = 1
W = 512
NBLK = 256
NL = 32768
B = 16


def draw_queries(key, part):
    count = NBLK * BLK
    span = H * E
    field = jnp.clip(jax.random.normal(jax.random.fold_in(key, 1), (count, span), jnp.float32), -5.0, 5.0)
    return field.astype(jnp.bfloat16)


def draw_keys(key, part):
    span = H * E
    field = jnp.clip(jax.random.normal(jax.random.fold_in(key, 2), (B, P_SIZE, span), jnp.float32), -5.0, 5.0)
    return field.astype(jnp.bfloat16)


def draw_block_mask(key, part):
    density = jax.random.randint(jax.random.fold_in(key, 3), (NBLK, 1), 1, 5)
    rolled = jax.random.randint(jax.random.fold_in(key, 4), (NBLK, B), 0, 4)
    return (rolled < density).astype(jnp.int32)


def level_of(stream_key, extent, split, low, high):
    gain = 1.0
    for dim, parts in split:
        draws = jax.random.uniform(jax.random.fold_in(jax.random.fold_in(stream_key, 6), dim), (parts,), jnp.float32, low / len(split), high / len(split))
        gain = gain * jnp.repeat(jnp.exp(draws), extent[dim] // parts).reshape((-1,) + (1,) * (len(extent) - 1 - dim))
    return gain


def scatter_about(stream_key, dims, deviation, limit, shards=(), held_as=jnp.bfloat16):
    entries = jax.random.normal(stream_key, dims, jnp.float32) * deviation
    if len(shards) > 0:
        entries = level_of(stream_key, dims, shards, -0.22, 0.18) * entries
    return jnp.clip(entries, min=-limit, max=limit).astype(held_as)


def setup_inputs(seed: int = 0) -> dict:
    arg_keys = jax.random.split(jax.random.key(seed), 6)
    return {
        "queries": draw_queries(jax.random.fold_in(arg_keys[5], 71), 0),
        "keys": draw_keys(jax.random.fold_in(arg_keys[5], 71), 0),
        "values": scatter_about(arg_keys[2], (B, P_SIZE, W), 1.0, 6.0, ((0, 16), (1, 32))),
        "grad_out": scatter_about(arg_keys[3], (B, NL, W), 1.0, 6.0, ((0, 16), (1, 32))),
        "block_mask": draw_block_mask(jax.random.fold_in(arg_keys[5], 71), 0),
    }


def attend_ref(query_block, grad_block, key_image, value_image, weight):
    scale = 1.0 / math.sqrt(E)
    scores = jnp.einsum('lhe,phe->lhp', query_block.astype(jnp.float32), key_image.astype(jnp.float32)) * scale
    probs = jax.nn.softmax(scores, axis=-1)
    dprobs = jnp.einsum('lhe,phe->lhp', grad_block.astype(jnp.float32), value_image.astype(jnp.float32))
    delta = lax.optimization_barrier(jnp.sum(probs * dprobs, axis=-1, keepdims=True))
    masked = (probs * weight).astype(jnp.bfloat16)
    dscores = (weight * probs * (dprobs - delta) * scale).astype(jnp.bfloat16)
    query_grad = jnp.einsum('lhp,phe->lhe', dscores.astype(jnp.float32), key_image.astype(jnp.float32))
    return (masked, dscores, query_grad)

def reference(queries, keys, values, grad_out, block_mask):
    groups = B // IMG_DEV
    query_blocks = queries.reshape(NBLK, BLK, H, E)
    weights = block_mask.astype(jnp.float32).T.reshape(groups, IMG_DEV, NBLK)
    keys_grp = keys.reshape(groups, IMG_DEV, P_SIZE, H, E)
    values_grp = values.reshape(groups, IMG_DEV, P_SIZE, H, E)
    grad_grp = grad_out.reshape(groups, IMG_DEV, NBLK, BLK, H, E)

    def per_image(partial_value, inputs):
        key_image, value_image, grad_image, weight_col = inputs

        def per_block(carry, pieces):
            dk_acc, dv_acc = carry
            query_block, grad_block, weight = pieces
            masked, dscores, query_grad = attend_ref(query_block, grad_block, key_image, value_image, weight)
            dk_acc = dk_acc + jnp.einsum('lhp,lhe->phe', dscores.astype(jnp.float32), query_block.astype(jnp.float32))
            dv_acc = dv_acc + jnp.einsum('lhp,lhe->phe', masked.astype(jnp.float32), grad_block.astype(jnp.float32))
            return ((dk_acc, dv_acc), query_grad)
        zero_acc = jnp.zeros((P_SIZE, H, E), jnp.float32)
        (dk_acc, dv_acc), query_grads = lax.scan(per_block, (zero_acc, zero_acc), (query_blocks, grad_image, weight_col))
        return (partial_value + query_grads, (dk_acc.astype(jnp.bfloat16).reshape(P_SIZE, H * E), dv_acc.astype(jnp.bfloat16).reshape(P_SIZE, H * E)))

    def per_group(total, inputs):
        start_sum = jnp.zeros((NBLK, BLK, H, E), jnp.float32)
        partial_value, pairs = lax.scan(per_image, start_sum, inputs)
        return (total + partial_value, pairs)
    total_init = jnp.zeros((NBLK, BLK, H, E), jnp.float32)
    total, (key_grad, value_grad) = lax.scan(per_group, total_init, (keys_grp, values_grp, grad_grp, weights))
    grad_queries = total.reshape(NBLK * BLK, H * E).astype(jnp.bfloat16)
    return (grad_queries, key_grad.reshape(B, P_SIZE, H * E), value_grad.reshape(B, P_SIZE, H * E))
```

```python
import functools
import math

import jax
import jax.numpy as jnp
from jax import lax
from jax.experimental import pallas as pl
from jax.experimental.pallas import tpu as pltpu
from jax.sharding import PartitionSpec as P

F32, BF16 = jnp.float32, jnp.bfloat16
MESH = pl.DeviceIdType.MESH
SCALE = 0.125
EXP2_SCALE = SCALE * math.log2(math.e)
PAIRS = 4
CH = 256
SIZES = (4, 4, 4, 4)


def dot(a, b, ca, cb):
    return lax.dot_general(a, b, (((ca,), (cb,)), ((), ())), preferred_element_type=F32)


def kernel(
    sizes,
    mask_ref,
    key_ref,
    val_ref,
    q_hbm,
    g_hbm,
    dq_out,
    dk_out,
    dv_out,
    q_v,
    g_v,
    kv,
    tl,
    tl_f,
    kt,
    acc,
    s_buf,
    d_buf,
    e_buf,
    mx_buf,
    dq_own,
    sx,
    rx,
    sz,
    rz,
    z_own,
    sa,
    ra,
    sb,
    rb,
    tb,
    sc,
    rc,
    st,
    rt,
    ft,
    in_sem,
    ag_send,
    ag_recv,
    agt_send,
    agt_recv,
    x_send,
    x_recv,
    h_send,
    h_recv,
    a_send,
    a_recv,
    b_send,
    b_recv,
    c_send,
    c_recv,
    t_send,
    t_recv,
):
    NZ, NY, NX, NH = sizes
    NS = NZ * NY
    NLAB = 2 * NS
    MAIN = 16 * NLAB
    ROWS = 18 * NLAB
    STEPS = PAIRS * NX
    HB = CH // NH
    ZR = NZ * 16
    HALF = NS * 16
    TH = NS * 2
    TZ = NZ * 2

    a = lax.axis_index("lab")
    i = lax.axis_index("img")
    z = a // (2 * NY)
    y = (a // 2) % NY
    c = a % 2
    x = i // NH
    zh = i % NH
    slot = c * NS + y * NZ + z

    def lab_id(z_, y_, c_):
        return {"lab": z_ * (2 * NY) + y_ * 2 + c_}

    def img_id(x_, h_):
        return {"img": x_ * NH + h_}

    def dev_z(d):
        return lab_id((z + d) % NZ, y, c)

    def dev_y(d):
        return lab_id(z, (y + d) % NY, c)

    def dev_c():
        return lab_id(z, y, 1 - c)

    def dev_x(d):
        return img_id((x + d) % NX, zh)

    def dev_h(d):
        return img_id(x, (zh + d) % NH)

    def rcopy(src, dst, ssem, rsem, dev):
        return pltpu.make_async_remote_copy(
            src_ref=src, dst_ref=dst, send_sem=ssem, recv_sem=rsem, device_id=dev, device_id_type=MESH
        )

    peers = [dev_c()]
    peers += [dev_z(d) for d in range(1, NZ)]
    peers += [dev_y(d) for d in range(1, NY)]
    peers += [dev_x(d) for d in range(1, NX)]
    peers += [dev_h(d) for d in range(1, NH)]
    barrier = pltpu.get_barrier_semaphore()
    for dev in peers:
        pl.semaphore_signal(barrier, inc=1, device_id=dev, device_id_type=MESH)

    def in_copies(j):
        lanes = pl.ds(pl.multiple_of(j * 128, 128), 128)
        return (
            pltpu.make_async_copy(q_hbm.at[:, lanes], q_v.at[j], in_sem.at[0, j]),
            pltpu.make_async_copy(g_hbm.at[0, :, lanes], g_v.at[j], in_sem.at[1, j]),
        )

    for j in range(PAIRS):
        for cp in in_copies(j):
            cp.start()

    for n, ref in ((0, key_ref), (1, val_ref)):
        for j in range(PAIRS):
            lanes = slice(j * 128, (j + 1) * 128)
            kv[j, n, pl.ds(pl.multiple_of(slot * 16, 16), 16), :] = ref[0, 0:16, lanes]
            tl_f[pl.ds(n * 8 + j * 2, 2), :] = ref[0, 16:18, lanes].astype(F32)
    tl[pl.ds(pl.multiple_of(slot * 16, 16), 16), :] = tl_f[...].astype(BF16)
    pl.semaphore_wait(barrier, len(peers))

    def ag_z(j, d):
        r = kv.at[j, :, pl.ds(pl.multiple_of(slot * 16, 16), 16), :]
        return rcopy(r, r, ag_send.at[j, d - 1], ag_recv.at[j, d - 1], dev_z(d))

    def ag_y(j, d):
        r = kv.at[j, :, pl.ds(pl.multiple_of(c * HALF + y * ZR, 16), ZR), :]
        n = NZ - 1 + d - 1
        return rcopy(r, r, ag_send.at[j, n], ag_recv.at[j, n], dev_y(d))

    def ag_c(j):
        r = kv.at[j, :, pl.ds(pl.multiple_of(c * HALF, 16), HALF), :]
        n = NZ + NY - 2
        return rcopy(r, r, ag_send.at[j, n], ag_recv.at[j, n], dev_c())

    def agt_z(d):
        r = tl.at[pl.ds(pl.multiple_of(slot * 16, 16), 16), :]
        return rcopy(r, r, agt_send.at[d - 1], agt_recv.at[d - 1], dev_z(d))

    def agt_y(d):
        r = tl.at[pl.ds(pl.multiple_of(c * HALF + y * ZR, 16), ZR), :]
        n = NZ - 1 + d - 1
        return rcopy(r, r, agt_send.at[n], agt_recv.at[n], dev_y(d))

    def agt_c():
        r = tl.at[pl.ds(pl.multiple_of(c * HALF, 16), HALF), :]
        n = NZ + NY - 2
        return rcopy(r, r, agt_send.at[n], agt_recv.at[n], dev_c())

    def z_to_y(j):
        for d in range(1, NZ):
            ag_z(j, d).wait_recv()
        for d in range(1, NY):
            ag_y(j, d).start()

    def y_to_c(j):
        for d in range(1, NY):
            ag_y(j, d).wait_recv()
        ag_c(j).start()

    for d in range(1, NZ):
        agt_z(d).start()
        ag_z(0, d).start()
    for j in range(1, PAIRS):
        for d in range(1, NZ):
            ag_z(j, d).start()

    for j in range(PAIRS):
        for n in range(2):
            acc[j, n] = jnp.zeros((ROWS, 128), F32)

    for d in range(1, NZ):
        agt_z(d).wait_recv()
    for d in range(1, NY):
        agt_y(d).start()
    z_to_y(0)
    z_to_y(1)
    tails = 16 * NLAB
    row = lax.broadcasted_iota(jnp.int32, (tails, tails), 0)
    col = lax.broadcasted_iota(jnp.int32, (tails, tails), 1)
    per = 2 * NLAB
    want = ((row % per) // 2) * 16 + ((row // per) % 2) * 8 + (row // (2 * per)) * 2 + row % 2
    order = jnp.where(col == want, 1.0, 0.0).astype(BF16)
    for d in range(1, NY):
        agt_y(d).wait_recv()
    agt_c().start()
    y_to_c(0)
    for j in range(2, PAIRS):
        z_to_y(j)
    agt_c().wait_recv()
    placed = dot(order, tl[...], 1, 0).astype(BF16)
    for j in range(PAIRS):
        for n in range(2):
            b0 = (j * 2 + n) * per
            kv[j, n, MAIN:ROWS, :] = placed[b0 : b0 + per, :]

    def turn_keys(j):
        kt[j] = jnp.transpose(kv[j, 0].astype(F32)).astype(BF16)

    def ready(j):
        ag_c(j).wait_recv()
        for cp in in_copies(j):
            cp.wait()
        turn_keys(j)

    ready(0)

    lane = lax.broadcasted_iota(jnp.int32, (1, 128), 1)

    def of_head(h, v):
        sel = (lane < 64) if h == 0 else (lane >= 64)
        return jnp.where(sel, v, jnp.zeros_like(v))

    def operands(s):
        s = s % STEPS
        j = s // NX
        chunk = (x + 1 + s % NX) % NX
        rows = pl.ds(pl.multiple_of(chunk * CH, CH), CH)
        return j, chunk, q_v[j, rows, :], g_v[j, rows, :]

    def front(s, h):
        j, _, q, g = operands(s)
        sv = dot(kv[j, 0], of_head(h, q), 1, 1)
        s_buf[h] = sv
        d_buf[h] = dot(kv[j, 1], of_head(h, g), 1, 1)
        mx_buf[h] = jnp.max(sv, axis=0, keepdims=True)

    def middle(h):
        e = jnp.exp2((s_buf[h] - mx_buf[h]) * EXP2_SCALE)
        e_buf[h] = e
        return jnp.sum(e, axis=0, keepdims=True), jnp.sum(e * d_buf[h], axis=0, keepdims=True)

    def back(h, j, q, g, m, total, weighted):
        qm, gm = of_head(h, q), of_head(h, g)
        t = e_buf[h] * (m / total)
        masked = t.astype(BF16)
        ds = (t * (d_buf[h] - weighted / total)).astype(BF16)
        acc[j, 0] += dot(ds, qm, 1, 0)
        acc[j, 1] += dot(masked, gm, 1, 0)
        return dot(kt[j, h * 64 : (h + 1) * 64, :], ds, 1, 0)

    def rs_a(j):
        return rcopy(sa.at[j], ra.at[j], a_send.at[j], a_recv.at[j], dev_c())

    def rs_b(j, d):
        return rcopy(sb.at[j, d - 1], rb.at[j, d - 1], b_send.at[j, d - 1], b_recv.at[j, d - 1], dev_y(d))

    def rs_c(j, d):
        return rcopy(sc.at[j, d - 1], rc.at[j, d - 1], c_send.at[j, d - 1], c_recv.at[j, d - 1], dev_z(d))

    def rs_t(d):
        return rcopy(st.at[(z + d) % NZ], rt.at[d - 1], t_send.at[d - 1], t_recv.at[d - 1], dev_z(d))

    def stage_a(j):
        other = 1 - c
        for n in range(2):
            sa[j, n, 0:HALF, :] = acc[j, n, pl.ds(pl.multiple_of(other * HALF, 16), HALF), :].astype(BF16)
            sa[j, n, HALF : HALF + TH, :] = acc[
                j, n, pl.ds(pl.multiple_of(MAIN + other * TH, 8), TH), :
            ].astype(BF16)
        rs_a(j).start()

    def stage_b(j):
        rs_a(j).wait_recv()
        for d in list(range(1, NY)) + [0]:
            yy = (y + d) % NY
            tail = []
            for n in range(2):
                at = pl.ds(pl.multiple_of(c * HALF + yy * ZR, 16), ZR)
                got = ra[j, n, pl.ds(pl.multiple_of(yy * ZR, 16), ZR), :].astype(F32)
                both = acc[j, n, at, :] + got
                tat = pl.ds(pl.multiple_of(MAIN + c * TH + yy * TZ, 8), TZ)
                tail.append(acc[j, n, tat, :])
                if d == 0:
                    acc[j, n, at, :] = both
                else:
                    sb[j, d - 1, n * ZR : (n + 1) * ZR, :] = both.astype(BF16)
            tmine = jnp.concatenate(tail, axis=0)
            for n in range(2):
                full = ra[j, n, HALF : HALF + TH, :].astype(F32)
                ft[n] = full
            tgot = jnp.concatenate(
                [ft[n, pl.ds(pl.multiple_of(yy * TZ, 8), TZ), :] for n in range(2)], axis=0
            )
            if d == 0:
                tb[j] = tmine + tgot
            else:
                sb[j, d - 1, 2 * ZR : 2 * ZR + 2 * TZ, :] = (tmine + tgot).astype(BF16)
                rs_b(j, d).start()

    def stage_c(j):
        for d in range(1, NY):
            rs_b(j, d).wait_recv()
        for n in range(2):
            at = pl.ds(pl.multiple_of(c * HALF + y * ZR, 16), ZR)
            v = acc[j, n, at, :]
            for d in range(1, NY):
                v = v + rb[j, d - 1, n * ZR : (n + 1) * ZR, :].astype(F32)
            acc[j, n, at, :] = v
        v = tb[j]
        for d in range(1, NY):
            v = v + rb[j, d - 1, 2 * ZR : 2 * ZR + 2 * TZ, :].astype(F32)
        tb[j] = v
        for d in range(1, NZ):
            zz = (z + d) % NZ
            for n in range(2):
                at = pl.ds(pl.multiple_of(c * HALF + y * ZR + zz * 16, 16), 16)
                sc[j, d - 1, n * 16 : (n + 1) * 16, :] = acc[j, n, at, :].astype(BF16)
            rs_c(j, d).start()

    def final_kv(j):
        for d in range(1, NZ):
            rs_c(j, d).wait_recv()
        lanes = pl.ds(pl.multiple_of(j * 128, 128), 128)
        for n, out in ((0, dk_out), (1, dv_out)):
            v = acc[j, n, pl.ds(pl.multiple_of(slot * 16, 16), 16), :]
            for d in range(1, NZ):
                v = v + rc[j, d - 1, n * 16 : (n + 1) * 16, :].astype(F32)
            if n == 0:
                v = v * SCALE
            out[0, 0:16, lanes] = v.astype(BF16)

    def rs_x(j, t):
        return rcopy(sx.at[j, t], rx.at[j, t], x_send.at[j, t], x_recv.at[j, t], dev_x(t + 1))

    def rs_h(j, d):
        return rcopy(sz.at[j, d - 1], rz.at[j, d - 1], h_send.at[j, d - 1], h_recv.at[j, d - 1], dev_h(d))

    def stage_h(j):
        for t in range(NX - 1):
            rs_x(j, t).wait_recv()
        v = dq_own[j]
        for t in range(NX - 1):
            v = v + rx[j, t].astype(F32)
        z_own[j] = jnp.transpose(v)
        for d in range(1, NH):
            hh = (zh + d) % NH
            sz[j, d - 1] = z_own[j, pl.ds(pl.multiple_of(hh * HB, HB), HB), :].astype(BF16)
            rs_h(j, d).start()

    def final_q(j):
        for d in range(1, NH):
            rs_h(j, d).wait_recv()
        v = z_own[j, pl.ds(pl.multiple_of(zh * HB, HB), HB), :]
        for d in range(1, NH):
            v = v + rz[j, d - 1].astype(F32)
        lanes = pl.ds(pl.multiple_of(j * 128, 128), 128)
        dq_out[:, lanes] = (v * SCALE).astype(BF16)

    front(0, 0)

    def body(s, carry):
        j = s // NX
        t = s % NX

        @pl.when(jnp.logical_and(t == min(1, NX - 2), j < PAIRS - 1))
        def _():
            y_to_c(j + 1)

        @pl.when(jnp.logical_and(t == NX - 1, j < PAIRS - 1))
        def _():
            ready(j + 1)

        _, chunk, q, g = operands(s)
        m = jnp.concatenate(
            [
                jnp.full((1, 128), mask_ref[chunk * (CH // 128) + b, 0], jnp.int32).astype(F32)
                for b in range(CH // 128)
            ],
            axis=1,
        )
        front(s, 1)
        total, weighted = middle(0)
        dq0 = back(0, j, q, g, m, total, weighted)
        front(s + 1, 0)
        total, weighted = middle(1)
        dq1 = back(1, j, q, g, m, total, weighted)

        @pl.when(t < NX - 1)
        def _():
            for u in range(NX - 1):

                @pl.when(t == u)
                def _():
                    sx[j, u, 0:64, :] = dq0.astype(BF16)
                    sx[j, u, 64:128, :] = dq1.astype(BF16)
                    rs_x(j, u).start()

        @pl.when(t == NX - 1)
        def _():
            dq_own[j, 0:64, :] = dq0
            dq_own[j, 64:128, :] = dq1
            stage_a(j)

        @pl.when(jnp.logical_and(t == 0, j > 0))
        def _():
            stage_h(j - 1)
            stage_b(j - 1)

        @pl.when(jnp.logical_and(t == max(NX - 2, 1), j > 0))
        def _():
            stage_c(j - 1)

        @pl.when(jnp.logical_and(t == NX - 1, j > 0))
        def _():
            final_kv(j - 1)
            final_q(j - 1)

        return carry

    lax.fori_loop(0, STEPS, body, 0)

    last = PAIRS - 1
    stage_h(last)
    stage_b(last)
    stage_c(last)
    n_t = PAIRS * 2 * TZ
    row = lax.broadcasted_iota(jnp.int32, (n_t, n_t), 0)
    col = lax.broadcasted_iota(jnp.int32, (n_t, n_t), 1)
    want = ((row // 4) % PAIRS) * (2 * TZ) + ((row // 2) % 2) * TZ + (row // 16) * 2 + row % 2
    order = jnp.where(col == want, 1.0, 0.0).astype(BF16)
    mine = jnp.concatenate([tb[j].astype(BF16) for j in range(PAIRS)], axis=0)
    sorted_tails = dot(order, mine, 1, 0).astype(BF16)
    for zz in range(NZ):
        st[zz] = sorted_tails[zz * 16 : (zz + 1) * 16, :]
    for d in range(1, NZ):
        rs_t(d).start()
    final_kv(last)
    for d in range(1, NZ):
        rs_t(d).wait_recv()
    v = st[z].astype(F32)
    for d in range(1, NZ):
        v = v + rt[d - 1].astype(F32)
    tl_f[...] = v
    for n, out in ((0, dk_out), (1, dv_out)):
        for j in range(PAIRS):
            piece = tl_f[pl.ds(j * 4 + n * 2, 2), :]
            if n == 0:
                piece = piece * SCALE
            out[0, 16:18, j * 128 : (j + 1) * 128] = piece.astype(BF16)
    final_q(last)

    for d in range(1, NZ):
        agt_z(d).wait_send()
        rs_t(d).wait_send()
    for d in range(1, NY):
        agt_y(d).wait_send()
    agt_c().wait_send()

    def drain(j, carry):
        for d in range(1, NZ):
            ag_z(j, d).wait_send()
            rs_c(j, d).wait_send()
        for d in range(1, NY):
            ag_y(j, d).wait_send()
            rs_b(j, d).wait_send()
        ag_c(j).wait_send()
        rs_a(j).wait_send()
        for t in range(NX - 1):
            rs_x(j, t).wait_send()
        for d in range(1, NH):
            rs_h(j, d).wait_send()
        return carry

    lax.fori_loop(0, PAIRS, drain, 0)


def body_of(sizes):
    NZ, NY, NX, NH = sizes
    NS = NZ * NY
    NLAB = 2 * NS
    ROWS = 18 * NLAB
    HB = CH // NH
    LABELS = CH * NX
    ZR, TZ = NZ * 16, NZ * 2
    dma = pltpu.SemaphoreType.DMA

    def body(queries, keys, values, grad_out, block_mask):
        vm = pl.BlockSpec(memory_space=pltpu.VMEM)
        sm = pl.BlockSpec(memory_space=pltpu.SMEM)
        anywhere = pl.BlockSpec(memory_space=pl.ANY)
        scratch = [
            pltpu.VMEM((PAIRS, LABELS, 128), BF16),
            pltpu.VMEM((PAIRS, LABELS, 128), BF16),
            pltpu.VMEM((PAIRS, 2, ROWS, 128), BF16),
            pltpu.VMEM((16 * NLAB, 128), BF16),
            pltpu.VMEM((16, 128), F32),
            pltpu.VMEM((PAIRS, 128, ROWS), BF16),
            pltpu.VMEM((PAIRS, 2, ROWS, 128), F32),
            pltpu.VMEM((2, ROWS, CH), F32),
            pltpu.VMEM((2, ROWS, CH), F32),
            pltpu.VMEM((2, ROWS, CH), F32),
            pltpu.VMEM((2, 1, CH), F32),
            pltpu.VMEM((PAIRS, 128, CH), F32),
            pltpu.VMEM((PAIRS, NX - 1, 128, CH), BF16),
            pltpu.VMEM((PAIRS, NX - 1, 128, CH), BF16),
            pltpu.VMEM((PAIRS, NH - 1, HB, 128), BF16),
            pltpu.VMEM((PAIRS, NH - 1, HB, 128), BF16),
            pltpu.VMEM((PAIRS, CH, 128), F32),
            pltpu.VMEM((PAIRS, 2, NS * 18, 128), BF16),
            pltpu.VMEM((PAIRS, 2, NS * 18, 128), BF16),
            pltpu.VMEM((PAIRS, NY - 1, 2 * ZR + 2 * TZ, 128), BF16),
            pltpu.VMEM((PAIRS, NY - 1, 2 * ZR + 2 * TZ, 128), BF16),
            pltpu.VMEM((PAIRS, 2 * TZ, 128), F32),
            pltpu.VMEM((PAIRS, NZ - 1, 32, 128), BF16),
            pltpu.VMEM((PAIRS, NZ - 1, 32, 128), BF16),
            pltpu.VMEM((NZ, 16, 128), BF16),
            pltpu.VMEM((NZ - 1, 16, 128), BF16),
            pltpu.VMEM((2, NS * 2, 128), F32),
            dma((2, PAIRS)),
            dma((PAIRS, NZ + NY - 1)),
            dma((PAIRS, NZ + NY - 1)),
            dma((NZ + NY - 1,)),
            dma((NZ + NY - 1,)),
            dma((PAIRS, NX - 1)),
            dma((PAIRS, NX - 1)),
            dma((PAIRS, NH - 1)),
            dma((PAIRS, NH - 1)),
            dma((PAIRS,)),
            dma((PAIRS,)),
            dma((PAIRS, NY - 1)),
            dma((PAIRS, NY - 1)),
            dma((PAIRS, NZ - 1)),
            dma((PAIRS, NZ - 1)),
            dma((NZ - 1,)),
            dma((NZ - 1,)),
        ]
        return pl.pallas_call(
            functools.partial(kernel, sizes),
            out_shape=(
                jax.ShapeDtypeStruct((HB, 512), BF16),
                jax.ShapeDtypeStruct((1, 18, 512), BF16),
                jax.ShapeDtypeStruct((1, 18, 512), BF16),
            ),
            in_specs=[sm, vm, vm, anywhere, anywhere],
            out_specs=(vm, vm, vm),
            scratch_shapes=scratch,
            compiler_params=pltpu.CompilerParams(
                collective_id=0, has_side_effects=True, vmem_limit_bytes=58 * 1024 * 1024
            ),
        )(block_mask, keys, values, queries, grad_out)

    return body


def build(mesh, sizes):
    return jax.shard_map(
        body_of(sizes),
        mesh=mesh,
        in_specs=(
            P("lab", None),
            P("img", "lab", None),
            P("img", "lab", None),
            P("img", "lab", None),
            P("lab", "img"),
        ),
        out_specs=(P(("lab", "img"), None), P("img", "lab", None), P("img", "lab", None)),
        check_vma=False,
    )


def solution(mesh):
    return build(mesh, SIZES)
```

```python
import functools
import math

import jax
import jax.numpy as jnp
from jax import lax
from jax.experimental import pallas as pl
from jax.experimental.pallas import tpu as pltpu
from jax.sharding import PartitionSpec as P

F32, BF16 = jnp.float32, jnp.bfloat16
MESH = pl.DeviceIdType.MESH
SCALE = 0.125
EXP2_SCALE = SCALE * math.log2(math.e)
PAIRS = 4
CH = 256
SIZES = (4, 4, 4, 4)


def dot(a, b, ca, cb):
    return lax.dot_general(a, b, (((ca,), (cb,)), ((), ())), preferred_element_type=F32)


def kernel(
    sizes,
    mask_ref,
    key_ref,
    val_ref,
    q_hbm,
    g_hbm,
    dq_out,
    dk_out,
    dv_out,
    q_v,
    g_v,
    kv,
    tl,
    tl_f,
    kt,
    acc,
    s_buf,
    d_buf,
    e_buf,
    mx_buf,
    dq_own,
    sx,
    rx,
    sz,
    rz,
    z_own,
    sa,
    ra,
    sb,
    rb,
    sc,
    rc,
    g0,
    sd,
    rd,
    in_order,
    out_order,
    in_sem,
    ag_send,
    ag_recv,
    g_send,
    g_recv,
    gc_send,
    gc_recv,
    x_send,
    x_recv,
    h_send,
    h_recv,
    a_send,
    a_recv,
    b_send,
    b_recv,
    c_send,
    c_recv,
    d_send,
    d_recv,
):
    NZ, NY, NX, NH = sizes
    NS = NZ * NY
    NLAB = 2 * NS
    MAIN = 16 * NLAB
    ROWS = 18 * NLAB
    STEPS = PAIRS * NX
    HB = CH // NH
    ZR = NZ * 16
    HALF = NS * 16
    TH = NS * 2
    BLOCK = 48
    last = PAIRS - 1

    a = lax.axis_index("lab")
    i = lax.axis_index("img")
    z = a // (2 * NY)
    y = (a // 2) % NY
    c = a % 2
    x = i // NH
    zh = i % NH
    slot = c * NS + y * NZ + z

    def lab_id(z_, y_, c_):
        return {"lab": z_ * (2 * NY) + y_ * 2 + c_}

    def img_id(x_, h_):
        return {"img": x_ * NH + h_}

    def dev_z(d):
        return lab_id((z + d) % NZ, y, c)

    def dev_y(d):
        return lab_id(z, (y + d) % NY, c)

    def dev_s(d):
        return lab_id((z + d % NZ) % NZ, (y + d // NZ) % NY, c)

    def dev_c():
        return lab_id(z, y, 1 - c)

    def dev_x(d):
        return img_id((x + d) % NX, zh)

    def dev_h(d):
        return img_id(x, (zh + d) % NH)

    def rcopy(src, dst, ssem, rsem, dev):
        return pltpu.make_async_remote_copy(
            src_ref=src, dst_ref=dst, send_sem=ssem, recv_sem=rsem, device_id=dev, device_id_type=MESH
        )

    peers = [dev_c()]
    peers += [dev_s(d) for d in range(1, NS)]
    peers += [dev_x(d) for d in range(1, NX)]
    peers += [dev_h(d) for d in range(1, NH)]
    barrier = pltpu.get_barrier_semaphore()
    for dev in peers:
        pl.semaphore_signal(barrier, inc=1, device_id=dev, device_id_type=MESH)

    def in_copies(j):
        lanes = pl.ds(pl.multiple_of(j * 128, 128), 128)
        return (
            pltpu.make_async_copy(q_hbm.at[:, lanes], q_v.at[j], in_sem.at[0, j]),
            pltpu.make_async_copy(g_hbm.at[0, :, lanes], g_v.at[j], in_sem.at[1, j]),
        )

    for j in range(PAIRS):
        for cp in in_copies(j):
            cp.start()

    mine = pl.multiple_of(slot * BLOCK, 16)
    for n, ref in ((0, key_ref), (1, val_ref)):
        for j in range(PAIRS):
            lanes = slice(j * 128, (j + 1) * 128)
            if j == 0:
                g0[pl.ds(mine + n * 16, 16), :] = ref[0, 0:16, lanes]
            else:
                kv[j, n, pl.ds(pl.multiple_of(slot * 16, 16), 16), :] = ref[0, 0:16, lanes]
            tl_f[pl.ds(n * 8 + j * 2, 2), :] = ref[0, 16:18, lanes].astype(F32)
    g0[pl.ds(mine + 32, 16), :] = tl_f[...].astype(BF16)

    per = 2 * NLAB
    row = lax.broadcasted_iota(jnp.int32, (16 * NLAB, 16 * NLAB), 0)
    col = lax.broadcasted_iota(jnp.int32, (16 * NLAB, 16 * NLAB), 1)
    want = ((row % per) // 2) * 16 + ((row // per) % 2) * 8 + (row // (2 * per)) * 2 + row % 2
    in_order[...] = jnp.where(col == want, 1.0, 0.0).astype(BF16)
    row = lax.broadcasted_iota(jnp.int32, (16 * NS, 16 * NS), 0)
    col = lax.broadcasted_iota(jnp.int32, (16 * NS, 16 * NS), 1)
    want = ((row // 4) % PAIRS) * (2 * TH) + ((row // 2) % 2) * TH + (row // 16) * 2 + row % 2
    out_order[...] = jnp.where(col == want, 1.0, 0.0).astype(BF16)
    for j in range(PAIRS):
        for n in range(2):
            acc[j, n] = jnp.zeros((ROWS, 128), F32)
    pl.semaphore_wait(barrier, len(peers))

    def ag_z(j, d):
        r = kv.at[j, :, pl.ds(pl.multiple_of(slot * 16, 16), 16), :]
        return rcopy(r, r, ag_send.at[j, d - 1], ag_recv.at[j, d - 1], dev_z(d))

    def ag_y(j, d):
        r = kv.at[j, :, pl.ds(pl.multiple_of(c * HALF + y * ZR, 16), ZR), :]
        n = NZ - 1 + d - 1
        return rcopy(r, r, ag_send.at[j, n], ag_recv.at[j, n], dev_y(d))

    def ag_c(j):
        r = kv.at[j, :, pl.ds(pl.multiple_of(c * HALF, 16), HALF), :]
        n = NZ + NY - 2
        return rcopy(r, r, ag_send.at[j, n], ag_recv.at[j, n], dev_c())

    def first_s(d):
        r = g0.at[pl.ds(mine, BLOCK), :]
        return rcopy(r, r, g_send.at[d - 1], g_recv.at[d - 1], dev_s(d))

    def first_c(d):
        yy = (y + NY - d) % NY
        r = g0.at[pl.ds(pl.multiple_of((c * NS + yy * NZ) * BLOCK, 16), NZ * BLOCK), :]
        return rcopy(r, r, gc_send.at[d], gc_recv.at[d], dev_c())

    def z_to_y(j):
        for d in range(1, NZ):
            ag_z(j, d).wait_recv()
        for d in range(1, NY):
            ag_y(j, d).start()

    def y_to_c(j):
        for d in range(1, NY):
            ag_y(j, d).wait_recv()
        ag_c(j).start()

    for d in range(1, NS):
        first_s(d).start()
    for j in range(1, PAIRS):
        for d in range(1, NZ):
            ag_z(j, d).start()
    for g in range(NY):
        for d in range(g * NZ, (g + 1) * NZ):
            if d > 0:
                first_s(d).wait_recv()
        first_c(g).start()
    for j in range(1, PAIRS):
        z_to_y(j)
    for g in range(NY):
        first_c(g).wait_recv()
    for n in range(NLAB):
        for u in range(2):
            kv[0, u, n * 16 : (n + 1) * 16, :] = g0[n * BLOCK + u * 16 : n * BLOCK + (u + 1) * 16, :]
        tl[n * 16 : (n + 1) * 16, :] = g0[n * BLOCK + 32 : (n + 1) * BLOCK, :]
    placed = dot(in_order[...], tl[...], 1, 0).astype(BF16)
    for j in range(PAIRS):
        for n in range(2):
            b0 = (j * 2 + n) * per
            kv[j, n, MAIN:ROWS, :] = placed[b0 : b0 + per, :]

    def turn_keys(j):
        kt[j] = jnp.transpose(kv[j, 0].astype(F32)).astype(BF16)

    def ready(j):
        for cp in in_copies(j):
            cp.wait()
        turn_keys(j)

    ready(0)

    lane = lax.broadcasted_iota(jnp.int32, (1, 128), 1)

    def of_head(h, v):
        sel = (lane < 64) if h == 0 else (lane >= 64)
        return jnp.where(sel, v, jnp.zeros_like(v))

    def operands(s):
        s = s % STEPS
        j = s // NX
        chunk = (x + 1 + s % NX) % NX
        rows = pl.ds(pl.multiple_of(chunk * CH, CH), CH)
        return j, chunk, q_v[j, rows, :], g_v[j, rows, :]

    def front(s, h):
        j, _, q, g = operands(s)
        sv = dot(kv[j, 0], of_head(h, q), 1, 1)
        s_buf[h] = sv
        d_buf[h] = dot(kv[j, 1], of_head(h, g), 1, 1)
        mx_buf[h] = jnp.max(sv, axis=0, keepdims=True)

    def middle(h):
        e = jnp.exp2((s_buf[h] - mx_buf[h]) * EXP2_SCALE)
        e_buf[h] = e
        return jnp.sum(e, axis=0, keepdims=True), jnp.sum(e * d_buf[h], axis=0, keepdims=True)

    def back(h, j, q, g, m, total, weighted):
        qm, gm = of_head(h, q), of_head(h, g)
        t = e_buf[h] * (m / total)
        masked = t.astype(BF16)
        ds = (t * (d_buf[h] - weighted / total)).astype(BF16)
        acc[j, 0] += dot(ds, qm, 1, 0)
        acc[j, 1] += dot(masked, gm, 1, 0)
        return dot(kt[j, h * 64 : (h + 1) * 64, :], ds, 1, 0)

    def rs_a(j):
        return rcopy(sa.at[j], ra.at[j], a_send.at[j], a_recv.at[j], dev_c())

    def rs_b(j, d):
        return rcopy(sb.at[j, d - 1], rb.at[j, d - 1], b_send.at[j, d - 1], b_recv.at[j, d - 1], dev_y(d))

    def rs_c(j, d):
        return rcopy(sc.at[j, d - 1], rc.at[j, d - 1], c_send.at[j, d - 1], c_recv.at[j, d - 1], dev_z(d))

    def rs_d(d):
        to = (y + d // NZ) % NY * NZ + (z + d % NZ) % NZ
        return rcopy(sd.at[to], rd.at[d - 1], d_send.at[d - 1], d_recv.at[d - 1], dev_s(d))

    def stage_a(j):
        other = 1 - c
        for n in range(2):
            sa[j, n, 0:HALF, :] = acc[j, n, pl.ds(pl.multiple_of(other * HALF, 16), HALF), :].astype(BF16)
            sa[j, n, HALF : HALF + TH, :] = acc[
                j, n, pl.ds(pl.multiple_of(MAIN + other * TH, 8), TH), :
            ].astype(BF16)
        rs_a(j).start()

    def stage_b(j):
        rs_a(j).wait_recv()
        for d in list(range(1, NY)) + [0]:
            yy = (y + d) % NY
            for n in range(2):
                at = pl.ds(pl.multiple_of(c * HALF + yy * ZR, 16), ZR)
                got = ra[j, n, pl.ds(pl.multiple_of(yy * ZR, 16), ZR), :].astype(F32)
                both = acc[j, n, at, :] + got
                if d == 0:
                    acc[j, n, at, :] = both
                else:
                    sb[j, d - 1, n * ZR : (n + 1) * ZR, :] = both.astype(BF16)
            if d > 0:
                rs_b(j, d).start()

    def stage_c(j):
        for d in range(1, NY):
            rs_b(j, d).wait_recv()
        for n in range(2):
            at = pl.ds(pl.multiple_of(c * HALF + y * ZR, 16), ZR)
            v = acc[j, n, at, :]
            for d in range(1, NY):
                v = v + rb[j, d - 1, n * ZR : (n + 1) * ZR, :].astype(F32)
            acc[j, n, at, :] = v
        for d in range(1, NZ):
            zz = (z + d) % NZ
            for n in range(2):
                at = pl.ds(pl.multiple_of(c * HALF + y * ZR + zz * 16, 16), 16)
                sc[j, d - 1, n * 16 : (n + 1) * 16, :] = acc[j, n, at, :].astype(BF16)
            rs_c(j, d).start()

    def stage_d():
        rs_a(last).wait_recv()
        tails = []
        for j in range(PAIRS):
            for n in range(2):
                t = acc[j, n, pl.ds(pl.multiple_of(MAIN + c * TH, 16), TH), :]
                tails.append((t + ra[j, n, HALF : HALF + TH, :].astype(F32)).astype(BF16))
        moved = dot(out_order[...], jnp.concatenate(tails, axis=0), 1, 0).astype(BF16)
        for n in range(2):
            at = pl.ds(pl.multiple_of(c * HALF, 16), HALF)
            v = acc[last, n, at, :] + ra[last, n, 0:HALF, :].astype(F32)
            acc[last, n, at, :] = v
            v = v.astype(BF16)
            for u in range(NS):
                sd[u, n * 16 : (n + 1) * 16, :] = v[u * 16 : (u + 1) * 16, :]
        for u in range(NS):
            sd[u, 32:48, :] = moved[u * 16 : (u + 1) * 16, :]
        for d in range(1, NS):
            rs_d(d).start()

    def final_d():
        for d in range(1, NS):
            rs_d(d).wait_recv()
        for n, out in ((0, dk_out), (1, dv_out)):
            v = acc[last, n, pl.ds(pl.multiple_of(slot * 16, 16), 16), :]
            for d in range(1, NS):
                v = v + rd[d - 1, n * 16 : (n + 1) * 16, :].astype(F32)
            if n == 0:
                v = v * SCALE
            out[0, 0:16, last * 128 : PAIRS * 128] = v.astype(BF16)
        v = sd[y * NZ + z, 32:48, :].astype(F32)
        for d in range(1, NS):
            v = v + rd[d - 1, 32:48, :].astype(F32)
        tl_f[...] = v
        for n, out in ((0, dk_out), (1, dv_out)):
            for j in range(PAIRS):
                piece = tl_f[pl.ds(j * 4 + n * 2, 2), :]
                if n == 0:
                    piece = piece * SCALE
                out[0, 16:18, j * 128 : (j + 1) * 128] = piece.astype(BF16)

    def final_kv(j):
        for d in range(1, NZ):
            rs_c(j, d).wait_recv()
        lanes = pl.ds(pl.multiple_of(j * 128, 128), 128)
        for n, out in ((0, dk_out), (1, dv_out)):
            v = acc[j, n, pl.ds(pl.multiple_of(slot * 16, 16), 16), :]
            for d in range(1, NZ):
                v = v + rc[j, d - 1, n * 16 : (n + 1) * 16, :].astype(F32)
            if n == 0:
                v = v * SCALE
            out[0, 0:16, lanes] = v.astype(BF16)

    def rs_x(j, t):
        return rcopy(sx.at[j, t], rx.at[j, t], x_send.at[j, t], x_recv.at[j, t], dev_x(t + 1))

    def rs_h(j, d):
        return rcopy(sz.at[j, d - 1], rz.at[j, d - 1], h_send.at[j, d - 1], h_recv.at[j, d - 1], dev_h(d))

    def stage_h(j):
        for t in range(NX - 1):
            rs_x(j, t).wait_recv()
        v = dq_own[j]
        for t in range(NX - 1):
            v = v + rx[j, t].astype(F32)
        z_own[j] = jnp.transpose(v)
        for d in range(1, NH):
            hh = (zh + d) % NH
            sz[j, d - 1] = z_own[j, pl.ds(pl.multiple_of(hh * HB, HB), HB), :].astype(BF16)
            rs_h(j, d).start()

    def final_q(j):
        for d in range(1, NH):
            rs_h(j, d).wait_recv()
        v = z_own[j, pl.ds(pl.multiple_of(zh * HB, HB), HB), :]
        for d in range(1, NH):
            v = v + rz[j, d - 1].astype(F32)
        lanes = pl.ds(pl.multiple_of(j * 128, 128), 128)
        dq_out[:, lanes] = (v * SCALE).astype(BF16)

    front(0, 0)

    def body(s, carry):
        j = s // NX
        t = s % NX

        @pl.when(jnp.logical_and(t == min(1, NX - 2), j < PAIRS - 1))
        def _():
            y_to_c(j + 1)

        @pl.when(jnp.logical_and(t == NX - 1, j < PAIRS - 1))
        def _():
            ag_c(j + 1).wait_recv()
            ready(j + 1)

        _, chunk, q, g = operands(s)
        m = jnp.concatenate(
            [
                jnp.full((1, 128), mask_ref[0, chunk * (CH // 128) + b], jnp.int32).astype(F32)
                for b in range(CH // 128)
            ],
            axis=1,
        )
        front(s, 1)
        total, weighted = middle(0)
        dq0 = back(0, j, q, g, m, total, weighted)
        front(s + 1, 0)
        total, weighted = middle(1)
        dq1 = back(1, j, q, g, m, total, weighted)

        @pl.when(t < NX - 1)
        def _():
            for u in range(NX - 1):

                @pl.when(t == u)
                def _():
                    sx[j, u, 0:64, :] = dq0.astype(BF16)
                    sx[j, u, 64:128, :] = dq1.astype(BF16)
                    rs_x(j, u).start()

        @pl.when(t == NX - 1)
        def _():
            dq_own[j, 0:64, :] = dq0
            dq_own[j, 64:128, :] = dq1
            stage_a(j)

        @pl.when(jnp.logical_and(t == min(1, NX - 1), j > 0))
        def _():
            stage_h(j - 1)
            stage_b(j - 1)

        @pl.when(jnp.logical_and(t == min(2, NX - 1), j > 1))
        def _():
            stage_c(j - 2)

        @pl.when(jnp.logical_and(t == NX - 1, j > 1))
        def _():
            final_q(j - 2)

        @pl.when(jnp.logical_and(t == NX - 1, j > 2))
        def _():
            final_kv(j - 3)

        return carry

    lax.fori_loop(0, STEPS, body, 0)

    stage_h(last)
    stage_d()
    stage_c(PAIRS - 2)
    final_kv(PAIRS - 3)
    final_q(PAIRS - 2)
    final_kv(PAIRS - 2)
    final_d()
    final_q(last)

    for d in range(1, NS):
        first_s(d).wait_send()
        rs_d(d).wait_send()
    for g in range(NY):
        first_c(g).wait_send()

    def drain(j, carry):
        rs_a(j).wait_send()
        for t in range(NX - 1):
            rs_x(j, t).wait_send()
        for d in range(1, NH):
            rs_h(j, d).wait_send()

        @pl.when(j > 0)
        def _():
            for d in range(1, NZ):
                ag_z(j, d).wait_send()
            for d in range(1, NY):
                ag_y(j, d).wait_send()
            ag_c(j).wait_send()

        @pl.when(j < last)
        def _():
            for d in range(1, NY):
                rs_b(j, d).wait_send()
            for d in range(1, NZ):
                rs_c(j, d).wait_send()

        return carry

    lax.fori_loop(0, PAIRS, drain, 0)


def body_of(sizes):
    NZ, NY, NX, NH = sizes
    NS = NZ * NY
    NLAB = 2 * NS
    ROWS = 18 * NLAB
    HB = CH // NH
    LABELS = CH * NX
    ZR = NZ * 16
    dma = pltpu.SemaphoreType.DMA

    def body(queries, keys, values, grad_out, block_mask):
        vm = pl.BlockSpec(memory_space=pltpu.VMEM)
        sm = pl.BlockSpec(memory_space=pltpu.SMEM)
        anywhere = pl.BlockSpec(memory_space=pl.ANY)
        scratch = [
            pltpu.VMEM((PAIRS, LABELS, 128), BF16),
            pltpu.VMEM((PAIRS, LABELS, 128), BF16),
            pltpu.VMEM((PAIRS, 2, ROWS, 128), BF16),
            pltpu.VMEM((16 * NLAB, 128), BF16),
            pltpu.VMEM((16, 128), F32),
            pltpu.VMEM((PAIRS, 128, ROWS), BF16),
            pltpu.VMEM((PAIRS, 2, ROWS, 128), F32),
            pltpu.VMEM((2, ROWS, CH), F32),
            pltpu.VMEM((2, ROWS, CH), F32),
            pltpu.VMEM((2, ROWS, CH), F32),
            pltpu.VMEM((2, 1, CH), F32),
            pltpu.VMEM((PAIRS, 128, CH), F32),
            pltpu.VMEM((PAIRS, NX - 1, 128, CH), BF16),
            pltpu.VMEM((PAIRS, NX - 1, 128, CH), BF16),
            pltpu.VMEM((PAIRS, NH - 1, HB, 128), BF16),
            pltpu.VMEM((PAIRS, NH - 1, HB, 128), BF16),
            pltpu.VMEM((PAIRS, CH, 128), F32),
            pltpu.VMEM((PAIRS, 2, NS * 18, 128), BF16),
            pltpu.VMEM((PAIRS, 2, NS * 18, 128), BF16),
            pltpu.VMEM((PAIRS, NY - 1, 2 * ZR, 128), BF16),
            pltpu.VMEM((PAIRS, NY - 1, 2 * ZR, 128), BF16),
            pltpu.VMEM((PAIRS, NZ - 1, 32, 128), BF16),
            pltpu.VMEM((PAIRS, NZ - 1, 32, 128), BF16),
            pltpu.VMEM((NLAB * 48, 128), BF16),
            pltpu.VMEM((NS, 48, 128), BF16),
            pltpu.VMEM((NS - 1, 48, 128), BF16),
            pltpu.VMEM((16 * NLAB, 16 * NLAB), BF16),
            pltpu.VMEM((16 * NS, 16 * NS), BF16),
            dma((2, PAIRS)),
            dma((PAIRS, NZ + NY - 1)),
            dma((PAIRS, NZ + NY - 1)),
            dma((NS - 1,)),
            dma((NS - 1,)),
            dma((NY,)),
            dma((NY,)),
            dma((PAIRS, NX - 1)),
            dma((PAIRS, NX - 1)),
            dma((PAIRS, NH - 1)),
            dma((PAIRS, NH - 1)),
            dma((PAIRS,)),
            dma((PAIRS,)),
            dma((PAIRS, NY - 1)),
            dma((PAIRS, NY - 1)),
            dma((PAIRS, NZ - 1)),
            dma((PAIRS, NZ - 1)),
            dma((NS - 1,)),
            dma((NS - 1,)),
        ]
        outs = pl.pallas_call(
            functools.partial(kernel, sizes),
            out_shape=(
                jax.ShapeDtypeStruct((HB, 512), BF16),
                jax.ShapeDtypeStruct((1, 18, 512), BF16),
                jax.ShapeDtypeStruct((1, 18, 512), BF16),
            ),
            in_specs=[sm, vm, vm, anywhere, anywhere],
            out_specs=(vm, vm, vm),
            scratch_shapes=scratch,
            compiler_params=pltpu.CompilerParams(
                collective_id=0, has_side_effects=True, vmem_limit_bytes=58 * 1024 * 1024
            ),
        )(block_mask.T, keys, values, queries, grad_out)
        return outs

    return body


def build(mesh, sizes):
    return jax.shard_map(
        body_of(sizes),
        mesh=mesh,
        in_specs=(
            P("lab", None),
            P("img", "lab", None),
            P("img", "lab", None),
            P("img", "lab", None),
            P("lab", "img"),
        ),
        out_specs=(P(("lab", "img"), None), P("img", "lab", None), P("img", "lab", None)),
        check_vma=False,
    )


def solution(mesh):
    return build(mesh, SIZES)
```

```python
import functools
import math

import jax
import jax.numpy as jnp
from jax import lax
from jax.experimental import pallas as pl
from jax.experimental.pallas import tpu as pltpu
from jax.sharding import PartitionSpec as P

F32, BF16 = jnp.float32, jnp.bfloat16
MESH = pl.DeviceIdType.MESH
SCALE = 0.125
EXP2_SCALE = SCALE * math.log2(math.e)
PAIRS = 4
CH = 256
SIZES = (4, 4, 4, 4)


def dot(a, b, ca, cb):
    return lax.dot_general(a, b, (((ca,), (cb,)), ((), ())), preferred_element_type=F32)


def kernel(
    sizes,
    mask_ref,
    key_hbm,
    val_hbm,
    q_hbm,
    g_hbm,
    dq_out,
    dk_out,
    dv_out,
    key_ref,
    val_ref,
    q_v,
    g_v,
    kv,
    tl,
    tl_f,
    kt,
    acc,
    s_buf,
    d_buf,
    e_buf,
    mx_buf,
    dq_own,
    sx,
    rx,
    sz,
    rz,
    z_own,
    sa,
    ra,
    sb,
    rb,
    sc,
    rc,
    g0,
    sd,
    rd,
    in_order,
    out_order,
    in_sem,
    kv_sem,
    ag_send,
    ag_recv,
    g_send,
    g_recv,
    gc_send,
    gc_recv,
    x_send,
    x_recv,
    h_send,
    h_recv,
    a_send,
    a_recv,
    b_send,
    b_recv,
    c_send,
    c_recv,
    d_send,
    d_recv,
):
    NZ, NY, NX, NH = sizes
    NS = NZ * NY
    NLAB = 2 * NS
    MAIN = 16 * NLAB
    ROWS = 18 * NLAB
    STEPS = PAIRS * NX
    HB = CH // NH
    ZR = NZ * 16
    HALF = NS * 16
    TH = NS * 2
    BLOCK = 48
    last = PAIRS - 1

    a = lax.axis_index("lab")
    i = lax.axis_index("img")
    z = a // (2 * NY)
    y = (a // 2) % NY
    c = a % 2
    x = i // NH
    zh = i % NH
    slot = c * NS + y * NZ + z

    def lab_id(z_, y_, c_):
        return {"lab": z_ * (2 * NY) + y_ * 2 + c_}

    def img_id(x_, h_):
        return {"img": x_ * NH + h_}

    def dev_z(d):
        return lab_id((z + d) % NZ, y, c)

    def dev_y(d):
        return lab_id(z, (y + d) % NY, c)

    def dev_s(d):
        return lab_id((z + d % NZ) % NZ, (y + d // NZ) % NY, c)

    def dev_c():
        return lab_id(z, y, 1 - c)

    def dev_x(d):
        return img_id((x + d) % NX, zh)

    def dev_h(d):
        return img_id(x, (zh + d) % NH)

    def rcopy(src, dst, ssem, rsem, dev):
        return pltpu.make_async_remote_copy(
            src_ref=src, dst_ref=dst, send_sem=ssem, recv_sem=rsem, device_id=dev, device_id_type=MESH
        )

    peers = [dev_c()]
    peers += [dev_s(d) for d in range(1, NS)]
    peers += [dev_x(d) for d in range(1, NX)]
    peers += [dev_h(d) for d in range(1, NH)]
    barrier = pltpu.get_barrier_semaphore()
    for dev in peers:
        pl.semaphore_signal(barrier, inc=1, device_id=dev, device_id_type=MESH)

    kv_copies = (
        pltpu.make_async_copy(key_hbm, key_ref, kv_sem.at[0]),
        pltpu.make_async_copy(val_hbm, val_ref, kv_sem.at[1]),
    )
    for cp in kv_copies:
        cp.start()

    def in_copies(j):
        lanes = pl.ds(pl.multiple_of(j * 128, 128), 128)
        return (
            pltpu.make_async_copy(q_hbm.at[:, lanes], q_v.at[j], in_sem.at[0, j]),
            pltpu.make_async_copy(g_hbm.at[0, :, lanes], g_v.at[j], in_sem.at[1, j]),
        )

    for j in range(PAIRS):
        for cp in in_copies(j):
            cp.start()

    per = 2 * NLAB

    def log2(n):
        return n.bit_length() - 1

    row = lax.broadcasted_iota(jnp.int32, (16 * NLAB, 1), 0)
    want = (
        (((row & (per - 1)) >> 1) << 4)
        + (((row >> log2(per)) & 1) << 3)
        + ((row >> log2(2 * per)) << 1)
        + (row & 1)
    )
    col = lax.broadcasted_iota(jnp.int32, (16 * NLAB, 16 * NLAB), 1)
    in_order[...] = jnp.where(col == want, 1.0, 0.0).astype(BF16)
    row = lax.broadcasted_iota(jnp.int32, (16 * NS, 1), 0)
    want = (
        (((row >> 2) & (PAIRS - 1)) << log2(2 * TH))
        + (((row >> 1) & 1) << log2(TH))
        + ((row >> 4) << 1)
        + (row & 1)
    )
    col = lax.broadcasted_iota(jnp.int32, (16 * NS, 16 * NS), 1)
    out_order[...] = jnp.where(col == want, 1.0, 0.0).astype(BF16)
    for cp in kv_copies:
        cp.wait()
    mine = pl.multiple_of(slot * BLOCK, 16)
    for n, ref in ((0, key_ref), (1, val_ref)):
        for j in range(PAIRS):
            lanes = slice(j * 128, (j + 1) * 128)
            if j == 0:
                g0[pl.ds(mine + n * 16, 16), :] = ref[0, 0:16, lanes]
            else:
                kv[j, n, pl.ds(pl.multiple_of(slot * 16, 16), 16), :] = ref[0, 0:16, lanes]
            tl_f[pl.ds(n * 8 + j * 2, 2), :] = ref[0, 16:18, lanes].astype(F32)
    g0[pl.ds(mine + 32, 16), :] = tl_f[...].astype(BF16)

    pl.semaphore_wait(barrier, len(peers))

    def ag_z(j, d):
        r = kv.at[j, :, pl.ds(pl.multiple_of(slot * 16, 16), 16), :]
        return rcopy(r, r, ag_send.at[j, d - 1], ag_recv.at[j, d - 1], dev_z(d))

    def ag_y(j, d):
        r = kv.at[j, :, pl.ds(pl.multiple_of(c * HALF + y * ZR, 16), ZR), :]
        n = NZ - 1 + d - 1
        return rcopy(r, r, ag_send.at[j, n], ag_recv.at[j, n], dev_y(d))

    def ag_c(j):
        r = kv.at[j, :, pl.ds(pl.multiple_of(c * HALF, 16), HALF), :]
        n = NZ + NY - 2
        return rcopy(r, r, ag_send.at[j, n], ag_recv.at[j, n], dev_c())

    def first_s(d):
        r = g0.at[pl.ds(mine, BLOCK), :]
        return rcopy(r, r, g_send.at[d - 1], g_recv.at[d - 1], dev_s(d))

    def first_c(d):
        yy = (y + NY - d) % NY
        r = g0.at[pl.ds(pl.multiple_of((c * NS + yy * NZ) * BLOCK, 16), NZ * BLOCK), :]
        return rcopy(r, r, gc_send.at[d], gc_recv.at[d], dev_c())

    def z_to_y(j):
        for d in range(1, NZ):
            ag_z(j, d).wait_recv()
        for d in range(1, NY):
            ag_y(j, d).start()

    def y_to_c(j):
        for d in range(1, NY):
            ag_y(j, d).wait_recv()
        ag_c(j).start()

    for d in range(1, NS):
        first_s(d).start()
    for d in range(1, NZ):
        ag_z(1, d).start()
    for g in range(NY):
        for d in range(g * NZ, (g + 1) * NZ):
            if d > 0:
                first_s(d).wait_recv()
        first_c(g).start()
    z_to_y(1)
    for j in range(2, PAIRS):
        for d in range(1, NZ):
            ag_z(j, d).start()
    for j in range(PAIRS):
        for n in range(2):
            acc[j, n] = jnp.zeros((ROWS, 128), F32)
    for g in range(NY):
        first_c(g).wait_recv()
    for n in range(NLAB):
        for u in range(2):
            kv[0, u, n * 16 : (n + 1) * 16, :] = g0[n * BLOCK + u * 16 : n * BLOCK + (u + 1) * 16, :]
        tl[n * 16 : (n + 1) * 16, :] = g0[n * BLOCK + 32 : (n + 1) * BLOCK, :]
    placed = dot(in_order[...], tl[...], 1, 0).astype(BF16)
    for j in range(PAIRS):
        for n in range(2):
            b0 = (j * 2 + n) * per
            kv[j, n, MAIN:ROWS, :] = placed[b0 : b0 + per, :]

    def turn_keys(j):
        kt[j] = jnp.transpose(kv[j, 0].astype(F32)).astype(BF16)

    def ready(j):
        for cp in in_copies(j):
            cp.wait()
        turn_keys(j)

    ready(0)

    lane = lax.broadcasted_iota(jnp.int32, (1, 128), 1)

    def of_head(h, v):
        sel = (lane < 64) if h == 0 else (lane >= 64)
        return jnp.where(sel, v, jnp.zeros_like(v))

    def operands(s):
        s = s % STEPS
        j = s // NX
        chunk = (x + 1 + s % NX) % NX
        rows = pl.ds(pl.multiple_of(chunk * CH, CH), CH)
        return j, chunk, q_v[j, rows, :], g_v[j, rows, :]

    def front(s, h):
        j, _, q, g = operands(s)
        sv = dot(kv[j, 0], of_head(h, q), 1, 1)
        s_buf[h] = sv
        d_buf[h] = dot(kv[j, 1], of_head(h, g), 1, 1)
        mx_buf[h] = jnp.max(sv, axis=0, keepdims=True)

    def middle(h):
        e = jnp.exp2((s_buf[h] - mx_buf[h]) * EXP2_SCALE)
        e_buf[h] = e
        return jnp.sum(e, axis=0, keepdims=True), jnp.sum(e * d_buf[h], axis=0, keepdims=True)

    def back(h, j, q, g, m, total, weighted):
        t = e_buf[h] * (m / total)
        masked = t.astype(BF16)
        ds = (t * (d_buf[h] - weighted / total)).astype(BF16)
        acc[j, 0] += dot(ds, of_head(h, q), 1, 0)
        acc[j, 1] += dot(masked, of_head(h, g), 1, 0)
        return dot(kt[j, h * 64 : (h + 1) * 64, :], ds, 1, 0)

    def rs_a(j):
        return rcopy(sa.at[j], ra.at[j], a_send.at[j], a_recv.at[j], dev_c())

    def rs_b(j, d):
        return rcopy(sb.at[j, d - 1], rb.at[j, d - 1], b_send.at[j, d - 1], b_recv.at[j, d - 1], dev_y(d))

    def rs_c(j, d):
        return rcopy(sc.at[j, d - 1], rc.at[j, d - 1], c_send.at[j, d - 1], c_recv.at[j, d - 1], dev_z(d))

    def rs_d(d):
        to = (y + d // NZ) % NY * NZ + (z + d % NZ) % NZ
        return rcopy(sd.at[to], rd.at[d - 1], d_send.at[d - 1], d_recv.at[d - 1], dev_s(d))

    def stage_a(j):
        other = 1 - c
        for n in range(2):
            sa[j, n, 0:HALF, :] = acc[j, n, pl.ds(pl.multiple_of(other * HALF, 16), HALF), :].astype(BF16)
            sa[j, n, HALF : HALF + TH, :] = acc[
                j, n, pl.ds(pl.multiple_of(MAIN + other * TH, 8), TH), :
            ].astype(BF16)
        rs_a(j).start()

    def stage_b(j):
        rs_a(j).wait_recv()
        for d in list(range(1, NY)) + [0]:
            yy = (y + d) % NY
            for n in range(2):
                at = pl.ds(pl.multiple_of(c * HALF + yy * ZR, 16), ZR)
                got = ra[j, n, pl.ds(pl.multiple_of(yy * ZR, 16), ZR), :].astype(F32)
                both = acc[j, n, at, :] + got
                if d == 0:
                    acc[j, n, at, :] = both
                else:
                    sb[j, d - 1, n * ZR : (n + 1) * ZR, :] = both.astype(BF16)
            if d > 0:
                rs_b(j, d).start()

    def stage_c(j):
        for d in range(1, NY):
            rs_b(j, d).wait_recv()
        for n in range(2):
            at = pl.ds(pl.multiple_of(c * HALF + y * ZR, 16), ZR)
            v = acc[j, n, at, :]
            for d in range(1, NY):
                v = v + rb[j, d - 1, n * ZR : (n + 1) * ZR, :].astype(F32)
            acc[j, n, at, :] = v
        for d in range(1, NZ):
            zz = (z + d) % NZ
            for n in range(2):
                at = pl.ds(pl.multiple_of(c * HALF + y * ZR + zz * 16, 16), 16)
                sc[j, d - 1, n * 16 : (n + 1) * 16, :] = acc[j, n, at, :].astype(BF16)
            rs_c(j, d).start()

    def stage_d():
        rs_a(last).wait_recv()
        tails = []
        for j in range(PAIRS):
            for n in range(2):
                t = acc[j, n, pl.ds(pl.multiple_of(MAIN + c * TH, 16), TH), :]
                tails.append((t + ra[j, n, HALF : HALF + TH, :].astype(F32)).astype(BF16))
        moved = dot(out_order[...], jnp.concatenate(tails, axis=0), 1, 0).astype(BF16)
        for n in range(2):
            at = pl.ds(pl.multiple_of(c * HALF, 16), HALF)
            v = acc[last, n, at, :] + ra[last, n, 0:HALF, :].astype(F32)
            acc[last, n, at, :] = v
            v = v.astype(BF16)
            for u in range(NS):
                sd[u, n * 16 : (n + 1) * 16, :] = v[u * 16 : (u + 1) * 16, :]
        for u in range(NS):
            sd[u, 32:48, :] = moved[u * 16 : (u + 1) * 16, :]
        for d in range(1, NS):
            rs_d(d).start()

    def final_d():
        for d in range(1, NS):
            rs_d(d).wait_recv()
        for n, out in ((0, dk_out), (1, dv_out)):
            v = acc[last, n, pl.ds(pl.multiple_of(slot * 16, 16), 16), :]
            for d in range(1, NS):
                v = v + rd[d - 1, n * 16 : (n + 1) * 16, :].astype(F32)
            if n == 0:
                v = v * SCALE
            out[0, 0:16, last * 128 : PAIRS * 128] = v.astype(BF16)
        v = sd[y * NZ + z, 32:48, :].astype(F32)
        for d in range(1, NS):
            v = v + rd[d - 1, 32:48, :].astype(F32)
        tl_f[...] = v
        for n, out in ((0, dk_out), (1, dv_out)):
            for j in range(PAIRS):
                piece = tl_f[pl.ds(j * 4 + n * 2, 2), :]
                if n == 0:
                    piece = piece * SCALE
                out[0, 16:18, j * 128 : (j + 1) * 128] = piece.astype(BF16)

    def final_kv(j):
        for d in range(1, NZ):
            rs_c(j, d).wait_recv()
        lanes = pl.ds(pl.multiple_of(j * 128, 128), 128)
        for n, out in ((0, dk_out), (1, dv_out)):
            v = acc[j, n, pl.ds(pl.multiple_of(slot * 16, 16), 16), :]
            for d in range(1, NZ):
                v = v + rc[j, d - 1, n * 16 : (n + 1) * 16, :].astype(F32)
            if n == 0:
                v = v * SCALE
            out[0, 0:16, lanes] = v.astype(BF16)

    def rs_x(j, t):
        return rcopy(sx.at[j, t], rx.at[j, t], x_send.at[j, t], x_recv.at[j, t], dev_x(t + 1))

    def rs_h(j, d):
        return rcopy(sz.at[j, d - 1], rz.at[j, d - 1], h_send.at[j, d - 1], h_recv.at[j, d - 1], dev_h(d))

    def stage_h(j):
        for t in range(NX - 1):
            rs_x(j, t).wait_recv()
        v = dq_own[j]
        for t in range(NX - 1):
            v = v + rx[j, t].astype(F32)
        z_own[j] = jnp.transpose(v)
        for d in range(1, NH):
            hh = (zh + d) % NH
            sz[j, d - 1] = z_own[j, pl.ds(pl.multiple_of(hh * HB, HB), HB), :].astype(BF16)
            rs_h(j, d).start()

    def final_q(j):
        for d in range(1, NH):
            rs_h(j, d).wait_recv()
        v = z_own[j, pl.ds(pl.multiple_of(zh * HB, HB), HB), :]
        for d in range(1, NH):
            v = v + rz[j, d - 1].astype(F32)
        lanes = pl.ds(pl.multiple_of(j * 128, 128), 128)
        dq_out[:, lanes] = (v * SCALE).astype(BF16)

    front(0, 0)

    def body(s, carry):
        j = s // NX
        t = s % NX

        @pl.when((t == min(2, NX - 2)) & (j < last))
        def _():
            y_to_c(j + 1)

        @pl.when((t == NX - 1) & (j < last))
        def _():
            ag_c(j + 1).wait_recv()
            ready(j + 1)

        _, chunk, q, g = operands(s)
        m = jnp.concatenate(
            [
                jnp.full((1, 128), mask_ref[0, chunk * (CH // 128) + b], jnp.int32).astype(F32)
                for b in range(CH // 128)
            ],
            axis=1,
        )
        front(s, 1)
        total, weighted = middle(0)
        dq0 = back(0, j, q, g, m, total, weighted)
        front(s + 1, 0)
        total, weighted = middle(1)
        dq1 = back(1, j, q, g, m, total, weighted)

        @pl.when(t < NX - 1)
        def _():
            for u in range(NX - 1):

                @pl.when(t == u)
                def _():
                    sx[j, u, 0:64, :] = dq0.astype(BF16)
                    sx[j, u, 64:128, :] = dq1.astype(BF16)
                    rs_x(j, u).start()

        @pl.when(t == NX - 1)
        def _():
            dq_own[j, 0:64, :] = dq0
            dq_own[j, 64:128, :] = dq1
            stage_a(j)

        @pl.when(jnp.logical_and(t == min(1, NX - 1), j > 0))
        def _():
            stage_h(j - 1)
            stage_b(j - 1)

        @pl.when(jnp.logical_and(t == min(2, NX - 1), j > 1))
        def _():
            stage_c(j - 2)

        @pl.when(jnp.logical_and(t == NX - 1, j > 1))
        def _():
            final_q(j - 2)

        @pl.when(jnp.logical_and(t == NX - 1, j > 2))
        def _():
            final_kv(j - 3)

        for k in range(2, PAIRS):

            @pl.when(s == min(k - 2, NX - 2))
            def _():
                z_to_y(k)

        return carry

    lax.fori_loop(0, STEPS, body, 0)

    stage_h(last)
    stage_d()
    stage_c(PAIRS - 2)
    final_kv(PAIRS - 3)
    final_q(PAIRS - 2)
    final_kv(PAIRS - 2)
    final_d()
    final_q(last)

    for d in range(1, NS):
        first_s(d).wait_send()
        rs_d(d).wait_send()
    for g in range(NY):
        first_c(g).wait_send()

    def drain(j, carry):
        rs_a(j).wait_send()
        for t in range(NX - 1):
            rs_x(j, t).wait_send()
        for d in range(1, NH):
            rs_h(j, d).wait_send()

        @pl.when(j > 0)
        def _():
            for d in range(1, NZ):
                ag_z(j, d).wait_send()
            for d in range(1, NY):
                ag_y(j, d).wait_send()
            ag_c(j).wait_send()

        @pl.when(j < last)
        def _():
            for d in range(1, NY):
                rs_b(j, d).wait_send()
            for d in range(1, NZ):
                rs_c(j, d).wait_send()

        return carry

    lax.fori_loop(0, PAIRS, drain, 0)


def body_of(sizes):
    NZ, NY, NX, NH = sizes
    NS = NZ * NY
    NLAB = 2 * NS
    ROWS = 18 * NLAB
    HB = CH // NH
    LABELS = CH * NX
    ZR = NZ * 16
    dma = pltpu.SemaphoreType.DMA

    def body(queries, keys, values, grad_out, block_mask):
        vm = pl.BlockSpec(memory_space=pltpu.VMEM)
        sm = pl.BlockSpec(memory_space=pltpu.SMEM)
        anywhere = pl.BlockSpec(memory_space=pl.ANY)
        scratch = [
            pltpu.VMEM((1, 18, 512), BF16),
            pltpu.VMEM((1, 18, 512), BF16),
            pltpu.VMEM((PAIRS, LABELS, 128), BF16),
            pltpu.VMEM((PAIRS, LABELS, 128), BF16),
            pltpu.VMEM((PAIRS, 2, ROWS, 128), BF16),
            pltpu.VMEM((16 * NLAB, 128), BF16),
            pltpu.VMEM((16, 128), F32),
            pltpu.VMEM((PAIRS, 128, ROWS), BF16),
            pltpu.VMEM((PAIRS, 2, ROWS, 128), F32),
            pltpu.VMEM((2, ROWS, CH), F32),
            pltpu.VMEM((2, ROWS, CH), F32),
            pltpu.VMEM((2, ROWS, CH), F32),
            pltpu.VMEM((2, 1, CH), F32),
            pltpu.VMEM((PAIRS, 128, CH), F32),
            pltpu.VMEM((PAIRS, NX - 1, 128, CH), BF16),
            pltpu.VMEM((PAIRS, NX - 1, 128, CH), BF16),
            pltpu.VMEM((PAIRS, NH - 1, HB, 128), BF16),
            pltpu.VMEM((PAIRS, NH - 1, HB, 128), BF16),
            pltpu.VMEM((PAIRS, CH, 128), F32),
            pltpu.VMEM((PAIRS, 2, NS * 18, 128), BF16),
            pltpu.VMEM((PAIRS, 2, NS * 18, 128), BF16),
            pltpu.VMEM((PAIRS, NY - 1, 2 * ZR, 128), BF16),
            pltpu.VMEM((PAIRS, NY - 1, 2 * ZR, 128), BF16),
            pltpu.VMEM((PAIRS, NZ - 1, 32, 128), BF16),
            pltpu.VMEM((PAIRS, NZ - 1, 32, 128), BF16),
            pltpu.VMEM((NLAB * 48, 128), BF16),
            pltpu.VMEM((NS, 48, 128), BF16),
            pltpu.VMEM((NS - 1, 48, 128), BF16),
            pltpu.VMEM((16 * NLAB, 16 * NLAB), BF16),
            pltpu.VMEM((16 * NS, 16 * NS), BF16),
            dma((2, PAIRS)),
            dma((2,)),
            dma((PAIRS, NZ + NY - 1)),
            dma((PAIRS, NZ + NY - 1)),
            dma((NS - 1,)),
            dma((NS - 1,)),
            dma((NY,)),
            dma((NY,)),
            dma((PAIRS, NX - 1)),
            dma((PAIRS, NX - 1)),
            dma((PAIRS, NH - 1)),
            dma((PAIRS, NH - 1)),
            dma((PAIRS,)),
            dma((PAIRS,)),
            dma((PAIRS, NY - 1)),
            dma((PAIRS, NY - 1)),
            dma((PAIRS, NZ - 1)),
            dma((PAIRS, NZ - 1)),
            dma((NS - 1,)),
            dma((NS - 1,)),
        ]
        outs = pl.pallas_call(
            functools.partial(kernel, sizes),
            out_shape=(
                pltpu.VMEM((HB, 512), BF16),
                pltpu.VMEM((1, 18, 512), BF16),
                pltpu.VMEM((1, 18, 512), BF16),
            ),
            in_specs=[sm, anywhere, anywhere, anywhere, anywhere],
            out_specs=(vm, vm, vm),
            scratch_shapes=scratch,
            compiler_params=pltpu.CompilerParams(
                collective_id=0, has_side_effects=True, vmem_limit_bytes=58 * 1024 * 1024
            ),
        )(block_mask.T, keys, values, queries, grad_out)
        return outs

    return body


def build(mesh, sizes):
    return jax.shard_map(
        body_of(sizes),
        mesh=mesh,
        in_specs=(
            P("lab", None),
            P("img", "lab", None),
            P("img", "lab", None),
            P("img", "lab", None),
            P("lab", "img"),
        ),
        out_specs=(P(("lab", "img"), None), P("img", "lab", None), P("img", "lab", None)),
        check_vma=False,
    )


def solution(mesh):
    return build(mesh, SIZES)
```

```python
import functools
import math

import jax
import jax.numpy as jnp
from jax import lax
from jax.experimental import pallas as pl
from jax.experimental.pallas import tpu as pltpu
from jax.sharding import PartitionSpec as P

F32, BF16 = jnp.float32, jnp.bfloat16
MESH = pl.DeviceIdType.MESH
SCALE = 0.125
EXP2_SCALE = SCALE * math.log2(math.e)
PAIRS = 4
CH = 256
SIZES = (4, 4, 4, 4)


def dot(a, b, ca, cb):
    return lax.dot_general(a, b, (((ca,), (cb,)), ((), ())), preferred_element_type=F32)


def kernel(
    sizes,
    mask_ref,
    key_hbm,
    val_hbm,
    q_hbm,
    g_hbm,
    dq_out,
    dk_out,
    dv_out,
    key_ref,
    val_ref,
    q_v,
    g_v,
    kv,
    tl,
    tl_f,
    kt,
    acc,
    s_buf,
    d_buf,
    e_buf,
    mx_buf,
    dq_own,
    sx,
    rx,
    sz,
    rz,
    z_own,
    sa,
    ra,
    sb,
    rb,
    sc,
    rc,
    g0,
    sd,
    rd,
    in_order,
    out_order,
    in_sem,
    kv_sem,
    ag_send,
    ag_recv,
    g_send,
    g_recv,
    gc_send,
    gc_recv,
    x_send,
    x_recv,
    h_send,
    h_recv,
    a_send,
    a_recv,
    b_send,
    b_recv,
    c_send,
    c_recv,
    d_send,
    d_recv,
    near_sem,
    far_sem,
):
    NZ, NY, NX, NH = sizes
    NS = NZ * NY
    NLAB = 2 * NS
    MAIN = 16 * NLAB
    ROWS = 18 * NLAB
    STEPS = PAIRS * NX
    HB = CH // NH
    ZR = NZ * 16
    HALF = NS * 16
    TH = NS * 2
    BLOCK = 48
    last = PAIRS - 1

    a = lax.axis_index("lab")
    i = lax.axis_index("img")
    z = a // (2 * NY)
    y = (a // 2) % NY
    c = a % 2
    x = i // NH
    zh = i % NH
    slot = c * NS + y * NZ + z

    def lab_id(z_, y_, c_):
        return {"lab": z_ * (2 * NY) + y_ * 2 + c_}

    def img_id(x_, h_):
        return {"img": x_ * NH + h_}

    def dev_z(d):
        return lab_id((z + d) % NZ, y, c)

    def dev_y(d):
        return lab_id(z, (y + d) % NY, c)

    def dev_s(d):
        return lab_id((z + d % NZ) % NZ, (y + d // NZ) % NY, c)

    def dev_c():
        return lab_id(z, y, 1 - c)

    def dev_x(d):
        return img_id((x + d) % NX, zh)

    def dev_h(d):
        return img_id(x, (zh + d) % NH)

    def rcopy(src, dst, ssem, rsem, dev):
        return pltpu.make_async_remote_copy(
            src_ref=src, dst_ref=dst, send_sem=ssem, recv_sem=rsem, device_id=dev, device_id_type=MESH
        )

    barrier = pltpu.get_barrier_semaphore()
    near = [lab_id((z + d % NZ) % NZ, (y + d // NZ) % NY, 0) for d in range(1, NS)]
    near += [{**lab_id(z, y, 0), **img_id((x + d) % NX, zh)} for d in range(1, NX)]
    far = [{**lab_id(z, y, 1), **img_id(x, (zh + d) % NH)} for d in range(1, NH)]
    for dev in near + far:
        pl.semaphore_signal(barrier, inc=1, device_id=dev, device_id_type=MESH)

    @pl.when(c == 1)
    def _():
        pl.semaphore_signal(barrier, inc=1, device_id=dev_c(), device_id_type=MESH)

    kv_copies = (
        pltpu.make_async_copy(key_hbm, key_ref, kv_sem.at[0]),
        pltpu.make_async_copy(val_hbm, val_ref, kv_sem.at[1]),
    )
    for cp in kv_copies:
        cp.start()

    def in_copies(j):
        lanes = pl.ds(pl.multiple_of(j * 128, 128), 128)
        return (
            pltpu.make_async_copy(q_hbm.at[:, lanes], q_v.at[j], in_sem.at[0, j]),
            pltpu.make_async_copy(g_hbm.at[0, :, lanes], g_v.at[j], in_sem.at[1, j]),
        )

    for j in range(PAIRS):
        for cp in in_copies(j):
            cp.start()

    per = 2 * NLAB

    def log2(n):
        return n.bit_length() - 1

    row = lax.broadcasted_iota(jnp.int32, (16 * NLAB, 1), 0)
    want = (
        (((row & (per - 1)) >> 1) << 4)
        + (((row >> log2(per)) & 1) << 3)
        + ((row >> log2(2 * per)) << 1)
        + (row & 1)
    )
    col = lax.broadcasted_iota(jnp.int32, (16 * NLAB, 16 * NLAB), 1)
    in_order[...] = jnp.where(col == want, 1.0, 0.0).astype(BF16)
    row = lax.broadcasted_iota(jnp.int32, (16 * NS, 1), 0)
    want = (
        (((row >> 2) & (PAIRS - 1)) << log2(2 * TH))
        + (((row >> 1) & 1) << log2(TH))
        + ((row >> 4) << 1)
        + (row & 1)
    )
    col = lax.broadcasted_iota(jnp.int32, (16 * NS, 16 * NS), 1)
    out_order[...] = jnp.where(col == want, 1.0, 0.0).astype(BF16)
    for cp in kv_copies:
        cp.wait()
    mine = pl.multiple_of(slot * BLOCK, 16)
    for n, ref in ((0, key_ref), (1, val_ref)):
        for j in range(PAIRS):
            lanes = slice(j * 128, (j + 1) * 128)
            if j == 0:
                g0[pl.ds(mine + n * 16, 16), :] = ref[0, 0:16, lanes]
            else:
                kv[j, n, pl.ds(pl.multiple_of(slot * 16, 16), 16), :] = ref[0, 0:16, lanes]
            tl_f[pl.ds(n * 8 + j * 2, 2), :] = ref[0, 16:18, lanes].astype(F32)
    g0[pl.ds(mine + 32, 16), :] = tl_f[...].astype(BF16)


    @pl.when(c == 0)
    def _():
        pl.semaphore_wait(barrier, 2 * len(near) + 1)
        pl.semaphore_signal(near_sem, inc=1, device_id=dev_c(), device_id_type=MESH)

    @pl.when(c == 1)
    def _():
        pl.semaphore_wait(near_sem, 1)

    def far_in():
        @pl.when(c == 1)
        def _():
            pl.semaphore_wait(barrier, 2 * len(far))
            pl.semaphore_signal(far_sem, inc=1, device_id=dev_c(), device_id_type=MESH)

        @pl.when(c == 0)
        def _():
            pl.semaphore_wait(far_sem, 1)

    def ag_z(j, d):
        r = kv.at[j, :, pl.ds(pl.multiple_of(slot * 16, 16), 16), :]
        return rcopy(r, r, ag_send.at[j, d - 1], ag_recv.at[j, d - 1], dev_z(d))

    def ag_y(j, d):
        r = kv.at[j, :, pl.ds(pl.multiple_of(c * HALF + y * ZR, 16), ZR), :]
        n = NZ - 1 + d - 1
        return rcopy(r, r, ag_send.at[j, n], ag_recv.at[j, n], dev_y(d))

    def ag_c(j):
        r = kv.at[j, :, pl.ds(pl.multiple_of(c * HALF, 16), HALF), :]
        n = NZ + NY - 2
        return rcopy(r, r, ag_send.at[j, n], ag_recv.at[j, n], dev_c())

    def first_s(d):
        r = g0.at[pl.ds(mine, BLOCK), :]
        return rcopy(r, r, g_send.at[d - 1], g_recv.at[d - 1], dev_s(d))

    def first_c(d):
        yy = (y + NY - d) % NY
        r = g0.at[pl.ds(pl.multiple_of((c * NS + yy * NZ) * BLOCK, 16), NZ * BLOCK), :]
        return rcopy(r, r, gc_send.at[d], gc_recv.at[d], dev_c())

    def z_to_y(j):
        for d in range(1, NZ):
            ag_z(j, d).wait_recv()
        for d in range(1, NY):
            ag_y(j, d).start()

    def y_to_c(j):
        for d in range(1, NY):
            ag_y(j, d).wait_recv()
        ag_c(j).start()

    for d in range(1, NS):
        first_s(d).start()
    for d in range(1, NZ):
        ag_z(1, d).start()
    for g in range(NY):
        for d in range(g * NZ, (g + 1) * NZ):
            if d > 0:
                first_s(d).wait_recv()
        first_c(g).start()
    z_to_y(1)
    for j in range(2, PAIRS):
        for d in range(1, NZ):
            ag_z(j, d).start()
    for j in range(PAIRS):
        for n in range(2):
            acc[j, n] = jnp.zeros((ROWS, 128), F32)
    for g in range(NY):
        first_c(g).wait_recv()
    for n in range(NLAB):
        for u in range(2):
            kv[0, u, n * 16 : (n + 1) * 16, :] = g0[n * BLOCK + u * 16 : n * BLOCK + (u + 1) * 16, :]
        tl[n * 16 : (n + 1) * 16, :] = g0[n * BLOCK + 32 : (n + 1) * BLOCK, :]
    placed = dot(in_order[...], tl[...], 1, 0).astype(BF16)
    for j in range(PAIRS):
        for n in range(2):
            b0 = (j * 2 + n) * per
            kv[j, n, MAIN:ROWS, :] = placed[b0 : b0 + per, :]

    def turn_keys(j):
        kt[j] = jnp.transpose(kv[j, 0].astype(F32)).astype(BF16)

    def ready(j):
        for cp in in_copies(j):
            cp.wait()
        turn_keys(j)

    ready(0)

    lane = lax.broadcasted_iota(jnp.int32, (1, 128), 1)

    def of_head(h, v):
        sel = (lane < 64) if h == 0 else (lane >= 64)
        return jnp.where(sel, v, jnp.zeros_like(v))

    def operands(s):
        s = s % STEPS
        j = s // NX
        chunk = (x + 1 + s % NX) % NX
        rows = pl.ds(pl.multiple_of(chunk * CH, CH), CH)
        return j, chunk, q_v[j, rows, :], g_v[j, rows, :]

    def front(s, h):
        j, _, q, g = operands(s)
        sv = dot(kv[j, 0], of_head(h, q), 1, 1)
        s_buf[h] = sv
        d_buf[h] = dot(kv[j, 1], of_head(h, g), 1, 1)
        mx_buf[h] = jnp.max(sv, axis=0, keepdims=True)

    def middle(h):
        e = jnp.exp2((s_buf[h] - mx_buf[h]) * EXP2_SCALE)
        e_buf[h] = e
        return jnp.sum(e, axis=0, keepdims=True), jnp.sum(e * d_buf[h], axis=0, keepdims=True)

    def back(h, j, q, g, m, total, weighted):
        t = e_buf[h] * (m / total)
        masked = t.astype(BF16)
        ds = (t * (d_buf[h] - weighted / total)).astype(BF16)
        acc[j, 0] += dot(ds, of_head(h, q), 1, 0)
        acc[j, 1] += dot(masked, of_head(h, g), 1, 0)
        return dot(kt[j, h * 64 : (h + 1) * 64, :], ds, 1, 0)

    def rs_a(j):
        return rcopy(sa.at[j], ra.at[j], a_send.at[j], a_recv.at[j], dev_c())

    def rs_b(j, d):
        return rcopy(sb.at[j, d - 1], rb.at[j, d - 1], b_send.at[j, d - 1], b_recv.at[j, d - 1], dev_y(d))

    def rs_c(j, d):
        return rcopy(sc.at[j, d - 1], rc.at[j, d - 1], c_send.at[j, d - 1], c_recv.at[j, d - 1], dev_z(d))

    def rs_d(d):
        to = (y + d // NZ) % NY * NZ + (z + d % NZ) % NZ
        return rcopy(sd.at[to], rd.at[d - 1], d_send.at[d - 1], d_recv.at[d - 1], dev_s(d))

    def stage_a(j):
        other = 1 - c
        for n in range(2):
            sa[j, n, 0:HALF, :] = acc[j, n, pl.ds(pl.multiple_of(other * HALF, 16), HALF), :].astype(BF16)
            sa[j, n, HALF : HALF + TH, :] = acc[
                j, n, pl.ds(pl.multiple_of(MAIN + other * TH, 8), TH), :
            ].astype(BF16)
        rs_a(j).start()

    def stage_b(j):
        rs_a(j).wait_recv()
        for d in list(range(1, NY)) + [0]:
            yy = (y + d) % NY
            for n in range(2):
                at = pl.ds(pl.multiple_of(c * HALF + yy * ZR, 16), ZR)
                got = ra[j, n, pl.ds(pl.multiple_of(yy * ZR, 16), ZR), :].astype(F32)
                both = acc[j, n, at, :] + got
                if d == 0:
                    acc[j, n, at, :] = both
                else:
                    sb[j, d - 1, n * ZR : (n + 1) * ZR, :] = both.astype(BF16)
            if d > 0:
                rs_b(j, d).start()

    def stage_c(j):
        for d in range(1, NY):
            rs_b(j, d).wait_recv()
        for n in range(2):
            at = pl.ds(pl.multiple_of(c * HALF + y * ZR, 16), ZR)
            v = acc[j, n, at, :]
            for d in range(1, NY):
                v = v + rb[j, d - 1, n * ZR : (n + 1) * ZR, :].astype(F32)
            acc[j, n, at, :] = v
        for d in range(1, NZ):
            zz = (z + d) % NZ
            for n in range(2):
                at = pl.ds(pl.multiple_of(c * HALF + y * ZR + zz * 16, 16), 16)
                sc[j, d - 1, n * 16 : (n + 1) * 16, :] = acc[j, n, at, :].astype(BF16)
            rs_c(j, d).start()

    def stage_d():
        rs_a(last).wait_recv()
        tails = []
        for j in range(PAIRS):
            for n in range(2):
                t = acc[j, n, pl.ds(pl.multiple_of(MAIN + c * TH, 16), TH), :]
                tails.append((t + ra[j, n, HALF : HALF + TH, :].astype(F32)).astype(BF16))
        moved = dot(out_order[...], jnp.concatenate(tails, axis=0), 1, 0).astype(BF16)
        for n in range(2):
            at = pl.ds(pl.multiple_of(c * HALF, 16), HALF)
            v = acc[last, n, at, :] + ra[last, n, 0:HALF, :].astype(F32)
            acc[last, n, at, :] = v
            v = v.astype(BF16)
            for u in range(NS):
                sd[u, n * 16 : (n + 1) * 16, :] = v[u * 16 : (u + 1) * 16, :]
        for u in range(NS):
            sd[u, 32:48, :] = moved[u * 16 : (u + 1) * 16, :]
        for d in range(1, NS):
            rs_d(d).start()

    def final_d():
        for d in range(1, NS):
            rs_d(d).wait_recv()
        for n, out in ((0, dk_out), (1, dv_out)):
            v = acc[last, n, pl.ds(pl.multiple_of(slot * 16, 16), 16), :]
            for d in range(1, NS):
                v = v + rd[d - 1, n * 16 : (n + 1) * 16, :].astype(F32)
            if n == 0:
                v = v * SCALE
            out[0, 0:16, last * 128 : PAIRS * 128] = v.astype(BF16)
        v = sd[y * NZ + z, 32:48, :].astype(F32)
        for d in range(1, NS):
            v = v + rd[d - 1, 32:48, :].astype(F32)
        tl_f[...] = v
        for n, out in ((0, dk_out), (1, dv_out)):
            for j in range(PAIRS):
                piece = tl_f[pl.ds(j * 4 + n * 2, 2), :]
                if n == 0:
                    piece = piece * SCALE
                out[0, 16:18, j * 128 : (j + 1) * 128] = piece.astype(BF16)

    def final_kv(j):
        for d in range(1, NZ):
            rs_c(j, d).wait_recv()
        lanes = pl.ds(pl.multiple_of(j * 128, 128), 128)
        for n, out in ((0, dk_out), (1, dv_out)):
            v = acc[j, n, pl.ds(pl.multiple_of(slot * 16, 16), 16), :]
            for d in range(1, NZ):
                v = v + rc[j, d - 1, n * 16 : (n + 1) * 16, :].astype(F32)
            if n == 0:
                v = v * SCALE
            out[0, 0:16, lanes] = v.astype(BF16)

    def rs_x(j, t):
        return rcopy(sx.at[j, t], rx.at[j, t], x_send.at[j, t], x_recv.at[j, t], dev_x(t + 1))

    def rs_h(j, d):
        return rcopy(sz.at[j, d - 1], rz.at[j, d - 1], h_send.at[j, d - 1], h_recv.at[j, d - 1], dev_h(d))

    def stage_h(j):
        for t in range(NX - 1):
            rs_x(j, t).wait_recv()
        v = dq_own[j]
        for t in range(NX - 1):
            v = v + rx[j, t].astype(F32)
        z_own[j] = jnp.transpose(v)
        for d in range(1, NH):
            hh = (zh + d) % NH
            sz[j, d - 1] = z_own[j, pl.ds(pl.multiple_of(hh * HB, HB), HB), :].astype(BF16)
            rs_h(j, d).start()

    def final_q(j):
        for d in range(1, NH):
            rs_h(j, d).wait_recv()
        v = z_own[j, pl.ds(pl.multiple_of(zh * HB, HB), HB), :]
        for d in range(1, NH):
            v = v + rz[j, d - 1].astype(F32)
        lanes = pl.ds(pl.multiple_of(j * 128, 128), 128)
        dq_out[:, lanes] = (v * SCALE).astype(BF16)

    front(0, 0)

    def body(s, carry):
        j = s // NX
        t = s % NX

        @pl.when((t == min(2, NX - 2)) & (j < last))
        def _():
            y_to_c(j + 1)

        @pl.when((t == NX - 1) & (j < last))
        def _():
            ag_c(j + 1).wait_recv()
            ready(j + 1)

        _, chunk, q, g = operands(s)
        m = jnp.concatenate(
            [
                jnp.full((1, 128), mask_ref[0, chunk * (CH // 128) + b], jnp.int32).astype(F32)
                for b in range(CH // 128)
            ],
            axis=1,
        )
        front(s, 1)
        total, weighted = middle(0)
        dq0 = back(0, j, q, g, m, total, weighted)
        front(s + 1, 0)
        total, weighted = middle(1)
        dq1 = back(1, j, q, g, m, total, weighted)

        @pl.when(t < NX - 1)
        def _():
            for u in range(NX - 1):

                @pl.when(t == u)
                def _():
                    sx[j, u, 0:64, :] = dq0.astype(BF16)
                    sx[j, u, 64:128, :] = dq1.astype(BF16)
                    rs_x(j, u).start()

        @pl.when(t == NX - 1)
        def _():
            dq_own[j, 0:64, :] = dq0
            dq_own[j, 64:128, :] = dq1
            stage_a(j)

        @pl.when(s == NX + min(1, NX - 1))
        def _():
            far_in()

        @pl.when(jnp.logical_and(t == min(1, NX - 1), j > 0))
        def _():
            stage_h(j - 1)
            stage_b(j - 1)

        @pl.when(jnp.logical_and(t == min(2, NX - 1), j > 1))
        def _():
            stage_c(j - 2)

        @pl.when(jnp.logical_and(t == NX - 1, j > 1))
        def _():
            final_q(j - 2)

        @pl.when(jnp.logical_and(t == NX - 1, j > 2))
        def _():
            final_kv(j - 3)

        for k in range(2, PAIRS):

            @pl.when(s == min(k - 2, NX - 2))
            def _():
                z_to_y(k)

        return carry

    lax.fori_loop(0, STEPS, body, 0)

    stage_h(last)
    stage_d()
    stage_c(PAIRS - 2)
    final_kv(PAIRS - 3)
    final_q(PAIRS - 2)
    final_kv(PAIRS - 2)
    final_d()
    final_q(last)

    for d in range(1, NS):
        first_s(d).wait_send()
        rs_d(d).wait_send()
    for g in range(NY):
        first_c(g).wait_send()

    def drain(j, carry):
        rs_a(j).wait_send()
        for t in range(NX - 1):
            rs_x(j, t).wait_send()
        for d in range(1, NH):
            rs_h(j, d).wait_send()

        @pl.when(j > 0)
        def _():
            for d in range(1, NZ):
                ag_z(j, d).wait_send()
            for d in range(1, NY):
                ag_y(j, d).wait_send()
            ag_c(j).wait_send()

        @pl.when(j < last)
        def _():
            for d in range(1, NY):
                rs_b(j, d).wait_send()
            for d in range(1, NZ):
                rs_c(j, d).wait_send()

        return carry

    lax.fori_loop(0, PAIRS, drain, 0)


def body_of(sizes):
    NZ, NY, NX, NH = sizes
    NS = NZ * NY
    NLAB = 2 * NS
    ROWS = 18 * NLAB
    HB = CH // NH
    LABELS = CH * NX
    ZR = NZ * 16
    dma = pltpu.SemaphoreType.DMA

    def body(queries, keys, values, grad_out, block_mask):
        vm = pl.BlockSpec(memory_space=pltpu.VMEM)
        sm = pl.BlockSpec(memory_space=pltpu.SMEM)
        anywhere = pl.BlockSpec(memory_space=pl.ANY)
        scratch = [
            pltpu.VMEM((1, 18, 512), BF16),
            pltpu.VMEM((1, 18, 512), BF16),
            pltpu.VMEM((PAIRS, LABELS, 128), BF16),
            pltpu.VMEM((PAIRS, LABELS, 128), BF16),
            pltpu.VMEM((PAIRS, 2, ROWS, 128), BF16),
            pltpu.VMEM((16 * NLAB, 128), BF16),
            pltpu.VMEM((16, 128), F32),
            pltpu.VMEM((PAIRS, 128, ROWS), BF16),
            pltpu.VMEM((PAIRS, 2, ROWS, 128), F32),
            pltpu.VMEM((2, ROWS, CH), F32),
            pltpu.VMEM((2, ROWS, CH), F32),
            pltpu.VMEM((2, ROWS, CH), F32),
            pltpu.VMEM((2, 1, CH), F32),
            pltpu.VMEM((PAIRS, 128, CH), F32),
            pltpu.VMEM((PAIRS, NX - 1, 128, CH), BF16),
            pltpu.VMEM((PAIRS, NX - 1, 128, CH), BF16),
            pltpu.VMEM((PAIRS, NH - 1, HB, 128), BF16),
            pltpu.VMEM((PAIRS, NH - 1, HB, 128), BF16),
            pltpu.VMEM((PAIRS, CH, 128), F32),
            pltpu.VMEM((PAIRS, 2, NS * 18, 128), BF16),
            pltpu.VMEM((PAIRS, 2, NS * 18, 128), BF16),
            pltpu.VMEM((PAIRS, NY - 1, 2 * ZR, 128), BF16),
            pltpu.VMEM((PAIRS, NY - 1, 2 * ZR, 128), BF16),
            pltpu.VMEM((PAIRS, NZ - 1, 32, 128), BF16),
            pltpu.VMEM((PAIRS, NZ - 1, 32, 128), BF16),
            pltpu.VMEM((NLAB * 48, 128), BF16),
            pltpu.VMEM((NS, 48, 128), BF16),
            pltpu.VMEM((NS - 1, 48, 128), BF16),
            pltpu.VMEM((16 * NLAB, 16 * NLAB), BF16),
            pltpu.VMEM((16 * NS, 16 * NS), BF16),
            dma((2, PAIRS)),
            dma((2,)),
            dma((PAIRS, NZ + NY - 1)),
            dma((PAIRS, NZ + NY - 1)),
            dma((NS - 1,)),
            dma((NS - 1,)),
            dma((NY,)),
            dma((NY,)),
            dma((PAIRS, NX - 1)),
            dma((PAIRS, NX - 1)),
            dma((PAIRS, NH - 1)),
            dma((PAIRS, NH - 1)),
            dma((PAIRS,)),
            dma((PAIRS,)),
            dma((PAIRS, NY - 1)),
            dma((PAIRS, NY - 1)),
            dma((PAIRS, NZ - 1)),
            dma((PAIRS, NZ - 1)),
            dma((NS - 1,)),
            dma((NS - 1,)),
            pltpu.SemaphoreType.REGULAR,
            pltpu.SemaphoreType.REGULAR,
        ]
        outs = pl.pallas_call(
            functools.partial(kernel, sizes),
            out_shape=(
                pltpu.VMEM((HB, 512), BF16),
                pltpu.VMEM((1, 18, 512), BF16),
                pltpu.VMEM((1, 18, 512), BF16),
            ),
            in_specs=[sm, anywhere, anywhere, anywhere, anywhere],
            out_specs=(vm, vm, vm),
            scratch_shapes=scratch,
            compiler_params=pltpu.CompilerParams(
                collective_id=0, has_side_effects=True, vmem_limit_bytes=58 * 1024 * 1024
            ),
        )(block_mask.T, keys, values, queries, grad_out)
        return outs

    return body


def build(mesh, sizes):
    return jax.shard_map(
        body_of(sizes),
        mesh=mesh,
        in_specs=(
            P("lab", None),
            P("img", "lab", None),
            P("img", "lab", None),
            P("img", "lab", None),
            P("lab", "img"),
        ),
        out_specs=(P(("lab", "img"), None), P("img", "lab", None), P("img", "lab", None)),
        check_vma=False,
    )


def solution(mesh):
    return build(mesh, SIZES)
```

```python
import functools
import math

import jax
import jax.numpy as jnp
from jax import lax
from jax.experimental import pallas as pl
from jax.experimental.pallas import tpu as pltpu
from jax.sharding import PartitionSpec as P

F32, BF16 = jnp.float32, jnp.bfloat16
MESH = pl.DeviceIdType.MESH
SCALE = 0.125
EXP2_SCALE = SCALE * math.log2(math.e)
PAIRS = 4
CH = 256
SIZES = (4, 4, 4, 4)


def dot(a, b, ca, cb):
    return lax.dot_general(a, b, (((ca,), (cb,)), ((), ())), preferred_element_type=F32)


def kernel(
    sizes,
    mask_ref,
    key_hbm,
    val_hbm,
    q_hbm,
    g_hbm,
    dq_out,
    dk_out,
    dv_out,
    key_ref,
    val_ref,
    q_v,
    g_v,
    kv,
    tl,
    tl_f,
    kt,
    acc,
    s_buf,
    d_buf,
    e_buf,
    mx_buf,
    dq_own,
    sx,
    rx,
    sz,
    rz,
    z_own,
    sa,
    ra,
    sb,
    rb,
    sc,
    rc,
    g0,
    sd,
    rd,
    in_order,
    out_order,
    in_sem,
    kv_sem,
    ag_send,
    ag_recv,
    g_send,
    g_recv,
    gc_send,
    gc_recv,
    x_send,
    x_recv,
    h_send,
    h_recv,
    a_send,
    a_recv,
    b_send,
    b_recv,
    c_send,
    c_recv,
    d_send,
    d_recv,
    near_sem,
    far_sem,
):
    NZ, NY, NX, NH = sizes
    NS = NZ * NY
    NLAB = 2 * NS
    MAIN = 16 * NLAB
    ROWS = 18 * NLAB
    STEPS = PAIRS * NX
    HB = CH // NH
    ZR = NZ * 16
    HALF = NS * 16
    TH = NS * 2
    BLOCK = 48
    last = PAIRS - 1

    a = lax.axis_index("lab")
    i = lax.axis_index("img")
    z = a // (2 * NY)
    y = (a // 2) % NY
    c = a % 2
    x = i // NH
    zh = i % NH
    slot = c * NS + y * NZ + z

    def lab_id(z_, y_, c_):
        return {"lab": z_ * (2 * NY) + y_ * 2 + c_}

    def img_id(x_, h_):
        return {"img": x_ * NH + h_}

    def dev_z(d):
        return lab_id((z + d) % NZ, y, c)

    def dev_y(d):
        return lab_id(z, (y + d) % NY, c)

    def dev_s(d):
        return lab_id((z + d % NZ) % NZ, (y + d // NZ) % NY, c)

    def dev_c():
        return lab_id(z, y, 1 - c)

    def dev_x(d):
        return img_id((x + d) % NX, zh)

    def dev_h(d):
        return img_id(x, (zh + d) % NH)

    def rcopy(src, dst, ssem, rsem, dev):
        return pltpu.make_async_remote_copy(
            src_ref=src, dst_ref=dst, send_sem=ssem, recv_sem=rsem, device_id=dev, device_id_type=MESH
        )

    barrier = pltpu.get_barrier_semaphore()
    near = [lab_id((z + d % NZ) % NZ, (y + d // NZ) % NY, 0) for d in range(1, NS)]
    near += [{**lab_id(z, y, 0), **img_id((x + d) % NX, zh)} for d in range(1, NX)]
    far = [{**lab_id(z, y, 1), **img_id(x, (zh + d) % NH)} for d in range(1, NH)]
    for dev in near + far:
        pl.semaphore_signal(barrier, inc=1, device_id=dev, device_id_type=MESH)

    @pl.when(c == 1)
    def _():
        pl.semaphore_signal(barrier, inc=1, device_id=dev_c(), device_id_type=MESH)

    kv_copies = (
        pltpu.make_async_copy(key_hbm, key_ref, kv_sem.at[0]),
        pltpu.make_async_copy(val_hbm, val_ref, kv_sem.at[1]),
    )
    for cp in kv_copies:
        cp.start()

    def in_copies(j):
        lanes = pl.ds(pl.multiple_of(j * 128, 128), 128)
        return (
            pltpu.make_async_copy(q_hbm.at[:, lanes], q_v.at[j], in_sem.at[0, j]),
            pltpu.make_async_copy(g_hbm.at[0, :, lanes], g_v.at[j], in_sem.at[1, j]),
        )

    for j in range(PAIRS):
        for cp in in_copies(j):
            cp.start()

    per = 2 * NLAB

    def log2(n):
        return n.bit_length() - 1

    row = lax.broadcasted_iota(jnp.int32, (16 * NLAB, 1), 0)
    want = (
        (((row & (per - 1)) >> 1) << 4)
        + (((row >> log2(per)) & 1) << 3)
        + ((row >> log2(2 * per)) << 1)
        + (row & 1)
    )
    col = lax.broadcasted_iota(jnp.int32, (16 * NLAB, 16 * NLAB), 1)
    in_order[...] = jnp.where(col == want, 1.0, 0.0).astype(BF16)
    row = lax.broadcasted_iota(jnp.int32, (16 * NS, 1), 0)
    want = (
        (((row >> 2) & (PAIRS - 1)) << log2(2 * TH))
        + (((row >> 1) & 1) << log2(TH))
        + ((row >> 4) << 1)
        + (row & 1)
    )
    col = lax.broadcasted_iota(jnp.int32, (16 * NS, 16 * NS), 1)
    out_order[...] = jnp.where(col == want, 1.0, 0.0).astype(BF16)
    for cp in kv_copies:
        cp.wait()
    mine = pl.multiple_of(slot * BLOCK, 16)
    for n, ref in ((0, key_ref), (1, val_ref)):
        for j in range(PAIRS):
            lanes = slice(j * 128, (j + 1) * 128)
            if j == 0:
                g0[pl.ds(mine + n * 16, 16), :] = ref[0, 0:16, lanes]
            else:
                kv[j, n, pl.ds(pl.multiple_of(slot * 16, 16), 16), :] = ref[0, 0:16, lanes]
            tl_f[pl.ds(n * 8 + j * 2, 2), :] = ref[0, 16:18, lanes].astype(F32)
    g0[pl.ds(mine + 32, 16), :] = tl_f[...].astype(BF16)


    @pl.when(c == 0)
    def _():
        pl.semaphore_wait(barrier, 2 * len(near) + 1)
        pl.semaphore_signal(near_sem, inc=1, device_id=dev_c(), device_id_type=MESH)

    @pl.when(c == 1)
    def _():
        pl.semaphore_wait(near_sem, 1)

    def far_in():
        @pl.when(c == 1)
        def _():
            pl.semaphore_wait(barrier, 2 * len(far))
            pl.semaphore_signal(far_sem, inc=1, device_id=dev_c(), device_id_type=MESH)

        @pl.when(c == 0)
        def _():
            pl.semaphore_wait(far_sem, 1)

    def ag_z(j, d):
        r = kv.at[j, :, pl.ds(pl.multiple_of(slot * 16, 16), 16), :]
        return rcopy(r, r, ag_send.at[j, d - 1], ag_recv.at[j, d - 1], dev_z(d))

    def ag_y(j, d):
        r = kv.at[j, :, pl.ds(pl.multiple_of(c * HALF + y * ZR, 16), ZR), :]
        n = NZ - 1 + d - 1
        return rcopy(r, r, ag_send.at[j, n], ag_recv.at[j, n], dev_y(d))

    def ag_c(j):
        r = kv.at[j, :, pl.ds(pl.multiple_of(c * HALF, 16), HALF), :]
        n = NZ + NY - 2
        return rcopy(r, r, ag_send.at[j, n], ag_recv.at[j, n], dev_c())

    def first_s(d):
        r = g0.at[pl.ds(mine, BLOCK), :]
        return rcopy(r, r, g_send.at[d - 1], g_recv.at[d - 1], dev_s(d))

    def first_c(d):
        yy = (y + NY - d) % NY
        r = g0.at[pl.ds(pl.multiple_of((c * NS + yy * NZ) * BLOCK, 16), NZ * BLOCK), :]
        return rcopy(r, r, gc_send.at[d], gc_recv.at[d], dev_c())

    def z_to_y(j):
        for d in range(1, NZ):
            ag_z(j, d).wait_recv()
        for d in range(1, NY):
            ag_y(j, d).start()

    def y_to_c(j):
        for d in range(1, NY):
            ag_y(j, d).wait_recv()
        ag_c(j).start()

    for d in range(1, NS):
        first_s(d).start()
    for d in range(1, NZ):
        ag_z(1, d).start()
    for g in range(NY):
        for d in range(g * NZ, (g + 1) * NZ):
            if d > 0:
                first_s(d).wait_recv()
        first_c(g).start()
    z_to_y(1)
    for j in range(2, PAIRS):
        for d in range(1, NZ):
            ag_z(j, d).start()
    for j in range(PAIRS):
        for n in range(2):
            acc[j, n] = jnp.zeros((ROWS, 128), F32)
    for g in range(NY):
        first_c(g).wait_recv()
    for n in range(NLAB):
        for u in range(2):
            kv[0, u, n * 16 : (n + 1) * 16, :] = g0[n * BLOCK + u * 16 : n * BLOCK + (u + 1) * 16, :]
        tl[n * 16 : (n + 1) * 16, :] = g0[n * BLOCK + 32 : (n + 1) * BLOCK, :]
    placed = dot(in_order[...], tl[...], 1, 0).astype(BF16)
    for j in range(PAIRS):
        for n in range(2):
            b0 = (j * 2 + n) * per
            kv[j, n, MAIN:ROWS, :] = placed[b0 : b0 + per, :]

    def turn_keys(j):
        kt[j] = jnp.transpose(kv[j, 0].astype(F32)).astype(BF16)

    def ready(j):
        for cp in in_copies(j):
            cp.wait()
        turn_keys(j)

    ready(0)

    lane = lax.broadcasted_iota(jnp.int32, (1, 128), 1)

    def of_head(h, v):
        sel = (lane < 64) if h == 0 else (lane >= 64)
        return jnp.where(sel, v, jnp.zeros_like(v))

    def operands(s):
        s = s % STEPS
        j = s // NX
        chunk = (x + 1 + s % NX) % NX
        rows = pl.ds(pl.multiple_of(chunk * CH, CH), CH)
        return j, chunk, q_v[j, rows, :], g_v[j, rows, :]

    def front(s, h):
        j, _, q, g = operands(s)
        sv = dot(kv[j, 0], of_head(h, q), 1, 1)
        s_buf[h] = sv
        d_buf[h] = dot(kv[j, 1], of_head(h, g), 1, 1)
        mx_buf[h] = jnp.max(sv, axis=0, keepdims=True)

    def middle(h):
        e = jnp.exp2((s_buf[h] - mx_buf[h]) * EXP2_SCALE)
        e_buf[h] = e
        return jnp.sum(e, axis=0, keepdims=True), jnp.sum(e * d_buf[h], axis=0, keepdims=True)

    def back(h, j, q, g, m, total, weighted):
        t = e_buf[h] * (m / total)
        masked = t.astype(BF16)
        ds = (t * (d_buf[h] - weighted / total)).astype(BF16)
        acc[j, 0] += dot(ds, of_head(h, q), 1, 0)
        acc[j, 1] += dot(masked, of_head(h, g), 1, 0)
        return dot(kt[j, h * 64 : (h + 1) * 64, :], ds, 1, 0)

    def rs_a(j):
        return rcopy(sa.at[j], ra.at[j], a_send.at[j], a_recv.at[j], dev_c())

    def rs_b(j, d):
        return rcopy(sb.at[j, d - 1], rb.at[j, d - 1], b_send.at[j, d - 1], b_recv.at[j, d - 1], dev_y(d))

    def rs_c(j, d):
        return rcopy(sc.at[j, d - 1], rc.at[j, d - 1], c_send.at[j, d - 1], c_recv.at[j, d - 1], dev_z(d))

    def rs_d(d):
        to = (y + d // NZ) % NY * NZ + (z + d % NZ) % NZ
        return rcopy(sd.at[to], rd.at[d - 1], d_send.at[d - 1], d_recv.at[d - 1], dev_s(d))

    def stage_a(j):
        other = 1 - c
        for n in range(2):
            sa[j, n, 0:HALF, :] = acc[j, n, pl.ds(pl.multiple_of(other * HALF, 16), HALF), :].astype(BF16)
            sa[j, n, HALF : HALF + TH, :] = acc[
                j, n, pl.ds(pl.multiple_of(MAIN + other * TH, 8), TH), :
            ].astype(BF16)
        rs_a(j).start()

    def stage_b(j):
        rs_a(j).wait_recv()
        for d in list(range(1, NY)) + [0]:
            yy = (y + d) % NY
            for n in range(2):
                at = pl.ds(pl.multiple_of(c * HALF + yy * ZR, 16), ZR)
                got = ra[j, n, pl.ds(pl.multiple_of(yy * ZR, 16), ZR), :].astype(F32)
                both = acc[j, n, at, :] + got
                if d == 0:
                    acc[j, n, at, :] = both
                else:
                    sb[j, d - 1, n * ZR : (n + 1) * ZR, :] = both.astype(BF16)
            if d > 0:
                rs_b(j, d).start()

    def stage_c(j):
        for d in range(1, NY):
            rs_b(j, d).wait_recv()
        for n in range(2):
            at = pl.ds(pl.multiple_of(c * HALF + y * ZR, 16), ZR)
            v = acc[j, n, at, :]
            for d in range(1, NY):
                v = v + rb[j, d - 1, n * ZR : (n + 1) * ZR, :].astype(F32)
            acc[j, n, at, :] = v
        for d in range(1, NZ):
            zz = (z + d) % NZ
            for n in range(2):
                at = pl.ds(pl.multiple_of(c * HALF + y * ZR + zz * 16, 16), 16)
                sc[j, d - 1, n * 16 : (n + 1) * 16, :] = acc[j, n, at, :].astype(BF16)
            rs_c(j, d).start()

    def stage_d():
        rs_a(last).wait_recv()
        tails = []
        for j in range(PAIRS):
            for n in range(2):
                t = acc[j, n, pl.ds(pl.multiple_of(MAIN + c * TH, 16), TH), :]
                tails.append((t + ra[j, n, HALF : HALF + TH, :].astype(F32)).astype(BF16))
        moved = dot(out_order[...], jnp.concatenate(tails, axis=0), 1, 0).astype(BF16)
        for n in range(2):
            at = pl.ds(pl.multiple_of(c * HALF, 16), HALF)
            v = acc[last, n, at, :] + ra[last, n, 0:HALF, :].astype(F32)
            acc[last, n, at, :] = v
            v = v.astype(BF16)
            for u in range(NS):
                sd[u, n * 16 : (n + 1) * 16, :] = v[u * 16 : (u + 1) * 16, :]
        for u in range(NS):
            sd[u, 32:48, :] = moved[u * 16 : (u + 1) * 16, :]
        for d in range(1, NS):
            rs_d(d).start()

    def final_d():
        for d in range(1, NS):
            rs_d(d).wait_recv()
        for n, out in ((0, dk_out), (1, dv_out)):
            v = acc[last, n, pl.ds(pl.multiple_of(slot * 16, 16), 16), :]
            for d in range(1, NS):
                v = v + rd[d - 1, n * 16 : (n + 1) * 16, :].astype(F32)
            if n == 0:
                v = v * SCALE
            out[0, 0:16, last * 128 : PAIRS * 128] = v.astype(BF16)
        v = sd[y * NZ + z, 32:48, :].astype(F32)
        for d in range(1, NS):
            v = v + rd[d - 1, 32:48, :].astype(F32)
        tl_f[...] = v
        for n, out in ((0, dk_out), (1, dv_out)):
            for j in range(PAIRS):
                piece = tl_f[pl.ds(j * 4 + n * 2, 2), :]
                if n == 0:
                    piece = piece * SCALE
                out[0, 16:18, j * 128 : (j + 1) * 128] = piece.astype(BF16)

    def final_kv(j):
        for d in range(1, NZ):
            rs_c(j, d).wait_recv()
        lanes = pl.ds(pl.multiple_of(j * 128, 128), 128)
        for n, out in ((0, dk_out), (1, dv_out)):
            v = acc[j, n, pl.ds(pl.multiple_of(slot * 16, 16), 16), :]
            for d in range(1, NZ):
                v = v + rc[j, d - 1, n * 16 : (n + 1) * 16, :].astype(F32)
            if n == 0:
                v = v * SCALE
            out[0, 0:16, lanes] = v.astype(BF16)

    def rs_x(j, t):
        return rcopy(sx.at[j, t], rx.at[j, t], x_send.at[j, t], x_recv.at[j, t], dev_x(t + 1))

    def rs_h(j, d):
        return rcopy(sz.at[j, d - 1], rz.at[j, d - 1], h_send.at[j, d - 1], h_recv.at[j, d - 1], dev_h(d))

    def stage_h(j):
        for t in range(NX - 1):
            rs_x(j, t).wait_recv()
        v = dq_own[j]
        for t in range(NX - 1):
            v = v + rx[j, t].astype(F32)
        z_own[j] = jnp.transpose(v)
        for d in range(1, NH):
            hh = (zh + d) % NH
            sz[j, d - 1] = z_own[j, pl.ds(pl.multiple_of(hh * HB, HB), HB), :].astype(BF16)
            rs_h(j, d).start()

    def final_q(j):
        for d in range(1, NH):
            rs_h(j, d).wait_recv()
        v = z_own[j, pl.ds(pl.multiple_of(zh * HB, HB), HB), :]
        for d in range(1, NH):
            v = v + rz[j, d - 1].astype(F32)
        lanes = pl.ds(pl.multiple_of(j * 128, 128), 128)
        dq_out[:, lanes] = (v * SCALE).astype(BF16)

    front(0, 0)

    def body(s, carry):
        j = s // NX
        t = s % NX

        @pl.when((t == min(2, NX - 2)) & (j < last))
        def _():
            y_to_c(j + 1)

        @pl.when((t == NX - 1) & (j < last))
        def _():
            ag_c(j + 1).wait_recv()
            ready(j + 1)

        _, chunk, q, g = operands(s)
        m = jnp.concatenate(
            [
                jnp.full((1, 128), mask_ref[0, chunk * (CH // 128) + b], jnp.int32).astype(F32)
                for b in range(CH // 128)
            ],
            axis=1,
        )
        front(s, 1)
        total, weighted = middle(0)
        dq0 = back(0, j, q, g, m, total, weighted)
        front(s + 1, 0)
        total, weighted = middle(1)
        dq1 = back(1, j, q, g, m, total, weighted)

        @pl.when(t < NX - 1)
        def _():
            for u in range(NX - 1):

                @pl.when(t == u)
                def _():
                    sx[j, u, 0:64, :] = dq0.astype(BF16)
                    sx[j, u, 64:128, :] = dq1.astype(BF16)
                    rs_x(j, u).start()

        @pl.when(t == NX - 1)
        def _():
            dq_own[j, 0:64, :] = dq0
            dq_own[j, 64:128, :] = dq1
            stage_a(j)

        @pl.when(jnp.logical_and(t == min(1, NX - 1), j > 0))
        def _():
            stage_b(j - 1)

        @pl.when(s == NX + min(2, NX - 1))
        def _():
            far_in()

        @pl.when(jnp.logical_and(t == min(2, NX - 1), j > 0))
        def _():
            stage_h(j - 1)

        @pl.when(jnp.logical_and(t == min(2, NX - 1), j > 1))
        def _():
            stage_c(j - 2)

        @pl.when(jnp.logical_and(t == NX - 1, j > 1))
        def _():
            final_q(j - 2)

        @pl.when(jnp.logical_and(t == NX - 1, j > 2))
        def _():
            final_kv(j - 3)

        for k in range(2, PAIRS):

            @pl.when(s == min(k - 2, NX - 2))
            def _():
                z_to_y(k)

        return carry

    lax.fori_loop(0, STEPS, body, 0)

    stage_h(last)
    stage_d()
    stage_c(PAIRS - 2)
    final_kv(PAIRS - 3)
    final_q(PAIRS - 2)
    final_kv(PAIRS - 2)
    final_d()
    final_q(last)

    for d in range(1, NS):
        first_s(d).wait_send()
        rs_d(d).wait_send()
    for g in range(NY):
        first_c(g).wait_send()

    def drain(j, carry):
        rs_a(j).wait_send()
        for t in range(NX - 1):
            rs_x(j, t).wait_send()
        for d in range(1, NH):
            rs_h(j, d).wait_send()

        @pl.when(j > 0)
        def _():
            for d in range(1, NZ):
                ag_z(j, d).wait_send()
            for d in range(1, NY):
                ag_y(j, d).wait_send()
            ag_c(j).wait_send()

        @pl.when(j < last)
        def _():
            for d in range(1, NY):
                rs_b(j, d).wait_send()
            for d in range(1, NZ):
                rs_c(j, d).wait_send()

        return carry

    lax.fori_loop(0, PAIRS, drain, 0)


def body_of(sizes):
    NZ, NY, NX, NH = sizes
    NS = NZ * NY
    NLAB = 2 * NS
    ROWS = 18 * NLAB
    HB = CH // NH
    LABELS = CH * NX
    ZR = NZ * 16
    dma = pltpu.SemaphoreType.DMA

    def body(queries, keys, values, grad_out, block_mask):
        vm = pl.BlockSpec(memory_space=pltpu.VMEM)
        sm = pl.BlockSpec(memory_space=pltpu.SMEM)
        anywhere = pl.BlockSpec(memory_space=pl.ANY)
        scratch = [
            pltpu.VMEM((1, 18, 512), BF16),
            pltpu.VMEM((1, 18, 512), BF16),
            pltpu.VMEM((PAIRS, LABELS, 128), BF16),
            pltpu.VMEM((PAIRS, LABELS, 128), BF16),
            pltpu.VMEM((PAIRS, 2, ROWS, 128), BF16),
            pltpu.VMEM((16 * NLAB, 128), BF16),
            pltpu.VMEM((16, 128), F32),
            pltpu.VMEM((PAIRS, 128, ROWS), BF16),
            pltpu.VMEM((PAIRS, 2, ROWS, 128), F32),
            pltpu.VMEM((2, ROWS, CH), F32),
            pltpu.VMEM((2, ROWS, CH), F32),
            pltpu.VMEM((2, ROWS, CH), F32),
            pltpu.VMEM((2, 1, CH), F32),
            pltpu.VMEM((PAIRS, 128, CH), F32),
            pltpu.VMEM((PAIRS, NX - 1, 128, CH), BF16),
            pltpu.VMEM((PAIRS, NX - 1, 128, CH), BF16),
            pltpu.VMEM((PAIRS, NH - 1, HB, 128), BF16),
            pltpu.VMEM((PAIRS, NH - 1, HB, 128), BF16),
            pltpu.VMEM((PAIRS, CH, 128), F32),
            pltpu.VMEM((PAIRS, 2, NS * 18, 128), BF16),
            pltpu.VMEM((PAIRS, 2, NS * 18, 128), BF16),
            pltpu.VMEM((PAIRS, NY - 1, 2 * ZR, 128), BF16),
            pltpu.VMEM((PAIRS, NY - 1, 2 * ZR, 128), BF16),
            pltpu.VMEM((PAIRS, NZ - 1, 32, 128), BF16),
            pltpu.VMEM((PAIRS, NZ - 1, 32, 128), BF16),
            pltpu.VMEM((NLAB * 48, 128), BF16),
            pltpu.VMEM((NS, 48, 128), BF16),
            pltpu.VMEM((NS - 1, 48, 128), BF16),
            pltpu.VMEM((16 * NLAB, 16 * NLAB), BF16),
            pltpu.VMEM((16 * NS, 16 * NS), BF16),
            dma((2, PAIRS)),
            dma((2,)),
            dma((PAIRS, NZ + NY - 1)),
            dma((PAIRS, NZ + NY - 1)),
            dma((NS - 1,)),
            dma((NS - 1,)),
            dma((NY,)),
            dma((NY,)),
            dma((PAIRS, NX - 1)),
            dma((PAIRS, NX - 1)),
            dma((PAIRS, NH - 1)),
            dma((PAIRS, NH - 1)),
            dma((PAIRS,)),
            dma((PAIRS,)),
            dma((PAIRS, NY - 1)),
            dma((PAIRS, NY - 1)),
            dma((PAIRS, NZ - 1)),
            dma((PAIRS, NZ - 1)),
            dma((NS - 1,)),
            dma((NS - 1,)),
            pltpu.SemaphoreType.REGULAR,
            pltpu.SemaphoreType.REGULAR,
        ]
        outs = pl.pallas_call(
            functools.partial(kernel, sizes),
            out_shape=(
                pltpu.VMEM((HB, 512), BF16),
                pltpu.VMEM((1, 18, 512), BF16),
                pltpu.VMEM((1, 18, 512), BF16),
            ),
            in_specs=[sm, anywhere, anywhere, anywhere, anywhere],
            out_specs=(vm, vm, vm),
            scratch_shapes=scratch,
            compiler_params=pltpu.CompilerParams(
                collective_id=0, has_side_effects=True, vmem_limit_bytes=58 * 1024 * 1024
            ),
        )(block_mask.T, keys, values, queries, grad_out)
        return outs

    return body


def build(mesh, sizes):
    return jax.shard_map(
        body_of(sizes),
        mesh=mesh,
        in_specs=(
            P("lab", None),
            P("img", "lab", None),
            P("img", "lab", None),
            P("img", "lab", None),
            P("lab", "img"),
        ),
        out_specs=(P(("lab", "img"), None), P("img", "lab", None), P("img", "lab", None)),
        check_vma=False,
    )


def solution(mesh):
    return build(mesh, SIZES)
```
